128 devices in a mesh: rows: 8 (over x_hi, y), cols: 16 (over x_lo, z, core).
Axes of the slice: x: 4 (x_hi: 2, x_lo: 2; x = x_hi * 2 + x_lo), y: 4, z: 4, core: 2. Of those that a mesh axis runs over, the one named last changes fastest.
Arguments:
- features: bfloat16 [3072, 4096, 32], P('rows', 'cols'), may hold values from -6 to 6
- conv_weight: bfloat16 [3, 3, 32, 128], replicated, may hold values from -0.375 to 0.375
- conv_bias: float32 [128], replicated, may hold values from -3 to 3
- head_weight: bfloat16 [128, 33], replicated, may hold values from -0.5 to 0.5
- head_bias: float32 [33], replicated, may hold values from -4 to 4
- tissue: int32 [8, 16], P('rows', 'cols'), may hold values 0 or 1
Outputs:
- probability: float32 [2048, 2048], P('rows', 'cols')
- ray_lengths: float32 [2048, 65536], P('rows', 'cols')
- peak_gap: float32 [2048, 2048], P('rows', 'cols')
The draws below stay inside these ranges and needn't reach their ends.
All inputs are finite; a program needn't handle non-finite values. No bound on the sum of `tissue` on one device may be relied on, other than what follows from the above.
Results may differ from the reference program's by a relative error of at most 0.0023.
Values may be sent and summed in bfloat16 or wider, within the bound.
No kernel may reach another device: no remote copies, remote signals or barrier semaphores. Data moves between devices by JAX's collectives and lax.ppermute only.
A program may use at most 192 MiB of HBM per device.

```python
import jax
import jax.numpy as jnp
from jax import lax

IN_CHANNELS = 32
CHANNELS = 128
RAYS = 32
MARGIN = 64
CORE_H = 256
CORE_W = 128
EXT_H = 384
EXT_W = 256
HEIGHT = 2048
WIDTH = 2048
N_ROWS = 8
N_COLS = 16


def set_ends(array, rng, smallest, top_value):
    longest = array.shape.index(max(array.shape))
    spots = []
    for shift in (0, 1):
        where = [jax.random.randint(jax.random.fold_in(rng, axis), (), 0, length) for axis, length in enumerate(array.shape)]
        where[longest] = (where[longest] + shift) % array.shape[longest]
        spots.append(tuple(where))
    return array.at[spots[0]].set(smallest).at[spots[1]].set(top_value)


def level_of(rng, dims, shards, smallest, high):
    factor_of = 1.0
    for position, blocks in shards:
        steps = jax.random.uniform(jax.random.fold_in(jax.random.fold_in(rng, 6), position), (blocks,), jnp.float32, smallest / len(shards), high / len(shards))
        factor_of = factor_of * jnp.repeat(jnp.exp(steps), dims[position] // blocks).reshape((-1,) + (1,) * (len(dims) - 1 - position))
    return factor_of


def gaussian(rng, shape, scale, bound, cuts=(), kind=jnp.bfloat16):
    values = scale * jax.random.normal(rng, shape, jnp.float32)
    if cuts:
        values = values * level_of(rng, shape, cuts, -0.22, 0.18)
    return jnp.clip(values, -bound, bound).astype(kind)


def setup_inputs(seed: int = 0) -> dict:
    seeds = jax.random.split(jax.random.key(seed), 7)
    return {
        "features": gaussian(seeds[0], (N_ROWS * EXT_H, N_COLS * EXT_W, IN_CHANNELS), 1.0, 6.0, ((0, 8), (1, 16))),
        "conv_weight": gaussian(seeds[1], (3, 3, IN_CHANNELS, CHANNELS), (9 * IN_CHANNELS) ** -0.5, 0.375),
        "conv_bias": gaussian(seeds[2], (CHANNELS,), 0.5, 3.0, (), jnp.float32),
        "head_weight": gaussian(seeds[3], (CHANNELS, RAYS + 1), CHANNELS ** -0.5, 0.5),
        "head_bias": gaussian(seeds[4], (RAYS + 1,), 1.0, 4.0, (), jnp.float32),
        "tissue": set_ends((jax.random.randint(seeds[5], (N_ROWS, N_COLS), 0, 2) < 1).astype(jnp.int32), jax.random.fold_in(seeds[5], 1), 0, 1),
    }


def local_gauss(extent):
    spread = jnp.float32(extent) / 4.0
    centred = jnp.arange(extent, dtype=jnp.int32).astype(jnp.float32) - (extent - 1) / 2.0
    return jnp.exp(-(centred * centred) / (2.0 * spread * spread))


def blend_total(positions, number, core_len, margin, extent):
    tile_ids = jnp.arange(number, dtype=jnp.int32)
    offsets = positions[None, :] - (tile_ids[:, None] * core_len - margin)
    covered = (offsets >= 0) & (offsets < extent)
    spread = jnp.float32(extent) / 4.0
    centred = offsets.astype(jnp.float32) - (extent - 1) / 2.0
    values = jnp.exp(-(centred * centred) / (2.0 * spread * spread))
    return jnp.sum(jnp.where(covered, values, jnp.float32(0.0)), axis=0)


def tile_output(window, conv_weight, conv_bias, head_weight, head_bias):
    summed = lax.conv_general_dilated(window[None].astype(jnp.float32), conv_weight.astype(jnp.float32), (1, 1), "SAME", dimension_numbers=("NHWC", "HWIO", "NHWC"), precision=lax.Precision.HIGHEST)[0]
    hidden = jnp.maximum(summed + conv_bias, 0.0).astype(jnp.bfloat16)
    channels = hidden.shape[-1]
    logits = jnp.dot(hidden.reshape(-1, channels), head_weight, preferred_element_type=jnp.float32) + head_bias
    outputs = jnp.concatenate([jax.nn.sigmoid(logits[:, :1]), logits[:, 1:]], axis=1)
    return outputs.T.reshape(-1, window.shape[0], window.shape[1])


def reference(features, conv_weight, conv_bias, head_weight, head_bias, tissue):
    tile_weight = local_gauss(EXT_H)[:, None] * local_gauss(EXT_W)[None, :]
    canvas = jnp.zeros((RAYS + 1, HEIGHT + 2 * MARGIN, WIDTH + 2 * MARGIN), jnp.float32)
    zero_index = jnp.zeros((), jnp.int32)

    def run_tile(window):
        return tile_output(window, conv_weight, conv_bias, head_weight, head_bias) * tile_weight

    def skip_tile(window):
        return jnp.zeros((RAYS + 1, EXT_H, EXT_W), jnp.float32)

    def add_tile(index, current):
        tile_row = (index // N_COLS).astype(jnp.int32)
        tile_col = (index % N_COLS).astype(jnp.int32)
        window = lax.dynamic_slice(features, (tile_row * EXT_H, tile_col * EXT_W, zero_index), (EXT_H, EXT_W, IN_CHANNELS))
        result = lax.cond(tissue[tile_row, tile_col] > 0, run_tile, skip_tile, window)
        corner = (zero_index, (tile_row * CORE_H).astype(jnp.int32), (tile_col * CORE_W).astype(jnp.int32))
        placed = lax.dynamic_slice(current, corner, (RAYS + 1, EXT_H, EXT_W))
        return lax.dynamic_update_slice(current, placed + result, corner)

    canvas = lax.fori_loop(0, N_ROWS * N_COLS, add_tile, canvas)
    numerator = canvas[:, MARGIN:MARGIN + HEIGHT, MARGIN:MARGIN + WIDTH]
    row_total = blend_total(jnp.arange(HEIGHT, dtype=jnp.int32), N_ROWS, CORE_H, MARGIN, EXT_H)
    col_total = blend_total(jnp.arange(WIDTH, dtype=jnp.int32), N_COLS, CORE_W, MARGIN, EXT_W)
    blended = numerator / (row_total[:, None] * col_total[None, :])[None]
    probability = blended[0]
    ray_lengths = jnp.transpose(blended[1:], (1, 2, 0)).reshape(HEIGHT, WIDTH * RAYS)
    rimmed = jnp.pad(probability, 2)
    window_max = lax.reduce_window(rimmed, -jnp.inf, lax.max, (5, 5), (1, 1), "VALID")
    return probability, ray_lengths, window_max - probability
```

```python
import functools

import jax
import jax.numpy as jnp
from jax import lax
from jax.experimental import pallas as pl
from jax.experimental.pallas import tpu as pltpu
from jax.sharding import PartitionSpec as P

MARGIN = 64
EXT_H, EXT_W = 384, 256
CORE_H, CORE_W = 256, 128
N_ROWS, N_COLS = 8, 16
CIN, COUT, RAYS = 32, 128, 32
M_PAIRS = 73
C_PAIRS = 128
M_OUT = 72
TAPS = 3 * CIN
F32, BF16 = jnp.float32, jnp.bfloat16


def lanes_of(shape):
    return lax.broadcasted_iota(jnp.int32, shape, len(shape) - 1)


def gauss(position, extent):
    spread = extent / 4.0
    centred = position.astype(F32) - (extent - 1) / 2.0
    return jnp.exp(-(centred * centred) / (2.0 * spread * spread))


def pack_pair(lo, hi, t, right_ref, left_ref, slot, extras):
    low_half = lanes_of((CIN, 128)) < 64
    spot = lanes_of((CIN, 128)) == t
    west_lo, east_lo = lo[:, :128], lo[:, 128:]
    west_hi, east_hi = hi[:, :128], hi[:, 128:]
    right_ref[slot] = jnp.where(low_half, pltpu.roll(east_lo, 64, 1), east_hi)
    left_ref[slot] = jnp.where(low_half, west_hi, pltpu.roll(west_lo, 64, 1))
    to_t_east = lax.rem(t + 128 - 63, 128)
    to_t_west = lax.rem(t + 128 - 64, 128)
    return (
        jnp.where(spot, pltpu.roll(east_lo, to_t_east, 1), extras[0]),
        jnp.where(spot, pltpu.roll(east_hi, to_t_east, 1), extras[1]),
        jnp.where(spot, pltpu.roll(west_lo, to_t_west, 1), extras[2]),
        jnp.where(spot, pltpu.roll(west_hi, to_t_west, 1), extras[3]),
    )


def pack_margin_kernel(tissue_ref, top_ref, bottom_ref, right_ref, left_ref):
    zero = jnp.zeros((CIN, 128), BF16)

    def step(t, extras):
        return pack_pair(top_ref[t], bottom_ref[95 - t], t, right_ref, left_ref, t, extras)

    extras = lax.fori_loop(0, M_PAIRS, step, (zero, zero, zero, zero))
    flag = jnp.where(tissue_ref[0, 0] > 0, 1.0, 0.0)
    flags = jnp.full((CIN, 128), flag, F32).astype(BF16)
    right_ref[M_PAIRS] = extras[0]
    right_ref[M_PAIRS + 1] = extras[1]
    right_ref[M_PAIRS + 2] = flags
    left_ref[M_PAIRS] = extras[2]
    left_ref[M_PAIRS + 1] = extras[3]
    left_ref[M_PAIRS + 2] = flags


def pack_margin(tissue, features):
    shape = jax.ShapeDtypeStruct((M_PAIRS + 3, CIN, 128), BF16)
    return pl.pallas_call(
        pack_margin_kernel,
        grid=(1,),
        in_specs=[
            pl.BlockSpec(memory_space=pltpu.SMEM),
            pl.BlockSpec((96, CIN, EXT_W), lambda s: (0, 0, 0)),
            pl.BlockSpec((96, CIN, EXT_W), lambda s: (3, 0, 0)),
        ],
        out_specs=[pl.BlockSpec(shape.shape, lambda s: (0, 0, 0))] * 2,
        out_shape=[shape, shape],
        compiler_params=pltpu.CompilerParams(vmem_limit_bytes=32 << 20),
        cost_estimate=pl.CostEstimate(flops=0, bytes_accessed=5 << 20, transcendentals=0),
    )(tissue, features, features)


def pack_core_kernel(low_ref, high_ref, right_ref, left_ref):
    zero = jnp.zeros((CIN, 128), BF16)

    def step(t, extras):
        q = lax.div(t, 64)
        s = lax.rem(t, 64)
        return pack_pair(
            low_ref[t], high_ref[127 - t], t, right_ref, left_ref, t, extras
        )

    extras = lax.fori_loop(0, C_PAIRS, step, (zero, zero, zero, zero))
    right_ref[C_PAIRS] = extras[0]
    right_ref[C_PAIRS + 1] = extras[1]
    left_ref[C_PAIRS] = extras[2]
    left_ref[C_PAIRS + 1] = extras[3]


def pack_core(features):
    shape = jax.ShapeDtypeStruct((C_PAIRS + 2, CIN, 128), BF16)
    core = features[MARGIN : EXT_H - MARGIN]
    return pl.pallas_call(
        pack_core_kernel,
        grid=(1,),
        in_specs=[
            pl.BlockSpec((128, CIN, EXT_W), lambda s: (0, 0, 0)),
            pl.BlockSpec((128, CIN, EXT_W), lambda s: (1, 0, 0)),
        ],
        out_specs=[pl.BlockSpec(shape.shape, lambda s: (0, 0, 0))] * 2,
        out_shape=[shape, shape],
        compiler_params=pltpu.CompilerParams(vmem_limit_bytes=32 << 20),
        cost_estimate=pl.CostEstimate(flops=0, bytes_accessed=6 << 20, transcendentals=0),
    )(core, core)


def column_taps(own, strip, from_west, from_east):
    lane = lanes_of((CIN, 128))
    west, east = own[:, :128], own[:, 128:]
    zero = jnp.zeros((CIN, 128), BF16)

    def own_tap(shift):
        amount = 64 - shift
        return jnp.where(lane < amount, pltpu.roll(west, amount, 1), pltpu.roll(east, amount, 1))

    strip_minus = jnp.where(
        lane == 0, from_west, jnp.where(lane == 64, zero, pltpu.roll(strip, 1, 1))
    )
    strip_plus = jnp.where(
        lane == 127, from_east, jnp.where(lane == 63, zero, pltpu.roll(strip, 127, 1))
    )
    return (
        jnp.concatenate([own_tap(-1), strip_minus], axis=1),
        jnp.concatenate([own_tap(0), strip], axis=1),
        jnp.concatenate([own_tap(1), strip_plus], axis=1),
    )


def build_pair(own_lo, own_hi, left, right, extras, t, taps_ref, lo_index, hi_index):
    low_half = lanes_of((CIN, 128)) < 64
    strip_lo = jnp.where(low_half, left, right)
    strip_hi = pltpu.roll(jnp.where(low_half, right, left), 64, 1)
    to_first = lax.rem(128 - t, 128)
    to_last = 127 - t
    for own, strip, west, east, index in (
        (own_lo, strip_lo, extras[0], extras[2], lo_index),
        (own_hi, strip_hi, extras[1], extras[3], hi_index),
    ):
        parts = column_taps(own, strip, pltpu.roll(west, to_first, 1), pltpu.roll(east, to_last, 1))
        start = pl.multiple_of(index * TAPS, 32)
        for k, part in enumerate(parts):
            taps_ref[pl.ds(start + k * CIN, CIN), :] = part


def prepare_weights(conv_ref, head_ref, bias_ref, conv_scr, head_scr):
    zero = jnp.zeros((TAPS, COUT), BF16)
    conv_scr[0 : 3 * TAPS, 0:COUT] = conv_ref[...]
    conv_scr[3 * TAPS : 4 * TAPS, 0:COUT] = zero
    conv_scr[0:TAPS, COUT:] = zero
    conv_scr[TAPS : 4 * TAPS, COUT:] = conv_ref[...]
    head = head_ref[...].astype(F32)
    head = jnp.concatenate([head, jnp.zeros((COUT - head.shape[0], COUT), F32)], axis=0).T
    lane = lanes_of((COUT, 128))
    for r in range(4):
        rays = pltpu.roll(head, (r * RAYS - 1) % 128, 1)
        rays = jnp.where((lane >= r * RAYS) & (lane < (r + 1) * RAYS), rays, 0.0)
        prob = jnp.where(lane == r, pltpu.roll(head, r, 1), 0.0)
        head_scr[r * COUT : (r + 1) * COUT, 0:128] = rays.astype(BF16)
        head_scr[r * COUT : (r + 1) * COUT, 128:256] = prob.astype(BF16)


def spread_bias(head_bias):
    lane = lanes_of((8, 128))
    rays = jnp.zeros((8, 128), F32)
    for r in range(4):
        moved = pltpu.roll(head_bias, (r * RAYS - 1) % 128, 1)
        rays = jnp.where((lane >= r * RAYS) & (lane < (r + 1) * RAYS), moved, rays)
    return rays[0:1]


def column_weights(tile_col, tissue, left_flags, right_flags):
    q = lax.broadcasted_iota(jnp.int32, (CORE_W, 128), 0)
    own = gauss(q + MARGIN, EXT_W)
    west = gauss(q + CORE_W + MARGIN, EXT_W)
    east = gauss(q - MARGIN, EXT_W)
    west_side = q < MARGIN
    has_west = jnp.where(tile_col > 0, 1.0, 0.0)
    has_east = jnp.where(tile_col < N_COLS - 1, 1.0, 0.0)
    side = jnp.where(west_side, west, east)
    total = own + side * jnp.where(west_side, has_west, has_east)
    flags = jnp.concatenate([left_flags, left_flags, right_flags, right_flags], axis=0)
    return own / total * jnp.where(tissue > 0, 1.0, 0.0), side / total * flags


def row_weights(row, tile_row):
    own = gauss(row, EXT_H)
    above = gauss(row + CORE_H, EXT_H) * jnp.where(tile_row > 0, 1.0, 0.0)
    below = gauss(row - CORE_H, EXT_H) * jnp.where(tile_row < N_ROWS - 1, 1.0, 0.0)
    total = own + jnp.where(row < 2 * MARGIN, above, 0.0) + jnp.where(row >= CORE_H, below, 0.0)
    return own / total


def group_logits(taps_ref, base, conv_scr, head_scr, bias):
    hidden = []
    for pair in range(2):
        start = pl.multiple_of((base + 2 * pair) * TAPS, 64)
        summed = lax.dot_general(
            taps_ref[pl.ds(start, 4 * TAPS), :],
            conv_scr[...],
            (((0,), (0,)), ((), ())),
            preferred_element_type=F32,
        )
        hidden.append(jnp.maximum(summed + bias, 0.0).astype(BF16))
    return jnp.dot(
        jnp.concatenate(hidden, axis=1), head_scr[...], preferred_element_type=F32
    )


def probability_block(logits, bias, first_row, tile_row, own_weight, side_weight):
    rows = lanes_of((CORE_W, 128)) + first_row
    values = 1.0 / (1.0 + jnp.exp(-(logits + bias)))
    return (values[:CORE_W] * own_weight + values[CORE_W:] * side_weight) * row_weights(
        rows, tile_row
    )


def margin_kernel(
    where_ref, tissue_ref, top_ref, bottom_ref, left_ref, right_ref,
    conv_ref, bias_ref, head_ref, hbias_ref,
    up_ref, down_ref, edge_ref,
    taps_ref, logit_ref, conv_scr, head_scr,
):
    tile_row, tile_col = where_ref[0], where_ref[1]
    prepare_weights(conv_ref, head_ref, bias_ref, conv_scr, head_scr)
    second = M_PAIRS + 1
    taps_ref[0:TAPS, :] = jnp.zeros((TAPS, 256), BF16)
    taps_ref[(2 * M_PAIRS + 1) * TAPS : (2 * M_PAIRS + 2) * TAPS, :] = jnp.zeros((TAPS, 256), BF16)
    extras = (left_ref[M_PAIRS], left_ref[M_PAIRS + 1], right_ref[M_PAIRS], right_ref[M_PAIRS + 1])

    def build(t, carry):
        build_pair(
            top_ref[t], bottom_ref[95 - t], left_ref[t], right_ref[t], extras, t,
            taps_ref, t + 1, second + 72 - t,
        )
        return carry

    lax.fori_loop(0, M_PAIRS, build, 0)
    own_weight, side_weight = column_weights(
        tile_col, tissue_ref[0, 0],
        left_ref[M_PAIRS + 2].astype(F32), right_ref[M_PAIRS + 2].astype(F32),
    )
    bias = jnp.concatenate([bias_ref[...], bias_ref[...]], axis=1)
    ray_bias = spread_bias(hbias_ref[...])
    logit_ref[...] = jnp.zeros(logit_ref.shape, F32)
    quarter = lax.div(lanes_of((1, 128)), RAYS)

    def compute(g, carry):
        for block, first_row, base in ((0, 0, 0), (1, 312, second)):
            logits = group_logits(taps_ref, base + 4 * g, conv_scr, head_scr, bias)
            factor = row_weights(first_row + 4 * g + quarter, tile_row)
            rays = (
                (logits[:CORE_W, :128] + ray_bias) * own_weight
                + (logits[CORE_W:, :128] + ray_bias) * side_weight
            ) * factor
            logit_ref[block] += pltpu.roll(logits[:, 128:], 4 * g, 1)
            if block == 0:
                @pl.when(g < 16)
                def _():
                    up_ref[pl.ds(pl.multiple_of(g * 128, 128), 128), :] = rays.astype(BF16)
            else:
                @pl.when(g >= 2)
                def _():
                    down_ref[pl.ds(pl.multiple_of((g - 2) * 128, 128), 128), :] = rays.astype(BF16)
        return carry

    lax.fori_loop(0, M_OUT // 4, compute, 0)
    for block, first_row, ref in ((0, 0, up_ref), (1, 312, down_ref)):
        prob = probability_block(
            logit_ref[block], hbias_ref[0, 0], first_row, tile_row, own_weight, side_weight
        )
        prob = jnp.where(lanes_of((CORE_W, 128)) < M_OUT, prob, 0.0)
        edge_ref[block] = prob
        high = prob.astype(BF16)
        ref[2048:2176, :] = high
        ref[2176:2304, :] = (prob - high.astype(F32)).astype(BF16)


def margin_outputs(where, tissue, features, left, right, weights):
    shape = jax.ShapeDtypeStruct((2304, 128), BF16)
    edge = jax.ShapeDtypeStruct((2, CORE_W, 128), F32)
    smem = pl.BlockSpec(memory_space=pltpu.SMEM)
    vmem = pl.BlockSpec(memory_space=pltpu.VMEM)
    return pl.pallas_call(
        margin_kernel,
        grid=(1,),
        in_specs=[
            smem, smem,
            pl.BlockSpec((96, CIN, EXT_W), lambda s: (0, 0, 0)),
            pl.BlockSpec((96, CIN, EXT_W), lambda s: (3, 0, 0)),
            vmem, vmem, vmem, vmem, vmem, vmem,
        ],
        out_specs=[vmem, vmem, vmem],
        out_shape=[shape, shape, edge],
        scratch_shapes=[
            pltpu.VMEM(((2 * M_PAIRS + 2) * TAPS, 256), BF16),
            pltpu.VMEM((2, 256, 128), F32),
            pltpu.VMEM((4 * TAPS, 256), BF16),
            pltpu.VMEM((4 * COUT, 256), BF16),
        ],
        compiler_params=pltpu.CompilerParams(vmem_limit_bytes=48 << 20),
        cost_estimate=pl.CostEstimate(flops=8 << 30, bytes_accessed=8 << 20, transcendentals=0),
    )(where, tissue, features, features, left, right, *weights)


def core_kernel(
    where_ref, tissue_ref, before_ref, low_ref, high_ref, after_ref, mleft_ref, mright_ref,
    left_ref, right_ref, conv_ref, bias_ref, head_ref, hbias_ref,
    rays_ref, prob_ref,
    taps_ref, logit_ref, conv_scr, head_scr,
):
    tile_row, tile_col = where_ref[0], where_ref[1]
    prepare_weights(conv_ref, head_ref, bias_ref, conv_scr, head_scr)
    extras = (mleft_ref[M_PAIRS], mleft_ref[M_PAIRS + 1], mright_ref[M_PAIRS], mright_ref[M_PAIRS + 1])
    build_pair(
        before_ref[0], after_ref[0], mleft_ref[63], mright_ref[63], extras, 63,
        taps_ref, 0, 257,
    )
    extras = (left_ref[C_PAIRS], left_ref[C_PAIRS + 1], right_ref[C_PAIRS], right_ref[C_PAIRS + 1])

    def build(t, carry):
        build_pair(
            low_ref[t], high_ref[127 - t], left_ref[t], right_ref[t], extras, t,
            taps_ref, 1 + t, 256 - t,
        )
        return carry

    lax.fori_loop(0, C_PAIRS, build, 0)
    own_weight, side_weight = column_weights(
        tile_col, tissue_ref[0, 0],
        mleft_ref[M_PAIRS + 2].astype(F32), mright_ref[M_PAIRS + 2].astype(F32),
    )
    bias = jnp.concatenate([bias_ref[...], bias_ref[...]], axis=1)
    ray_bias = spread_bias(hbias_ref[...])
    logit_ref[...] = jnp.zeros(logit_ref.shape, F32)
    quarter = lax.div(lanes_of((1, 128)), RAYS)

    def compute(h, carry):
        for block in range(2):
            g = block * 32 + h
            logits = group_logits(taps_ref, 4 * g, conv_scr, head_scr, bias)
            factor = row_weights(MARGIN + 4 * g + quarter, tile_row)
            rays = (
                (logits[:CORE_W, :128] + ray_bias) * own_weight
                + (logits[CORE_W:, :128] + ray_bias) * side_weight
            ) * factor
            rays_ref[g] = rays
            logit_ref[block] += pltpu.roll(logits[:, 128:], 4 * h, 1)
        return carry

    lax.fori_loop(0, 32, compute, 0)
    for block in range(2):
        prob_ref[block] = probability_block(
            logit_ref[block], hbias_ref[0, 0], MARGIN + 128 * block, tile_row,
            own_weight, side_weight,
        )


def core_outputs(where, tissue, features, mleft, mright, left, right, weights):
    smem = pl.BlockSpec(memory_space=pltpu.SMEM)
    vmem = pl.BlockSpec(memory_space=pltpu.VMEM)
    core = features[MARGIN : EXT_H - MARGIN]
    return pl.pallas_call(
        core_kernel,
        grid=(1,),
        in_specs=[
            smem, smem,
            pl.BlockSpec((1, CIN, EXT_W), lambda s: (63, 0, 0)),
            pl.BlockSpec((128, CIN, EXT_W), lambda s: (0, 0, 0)),
            pl.BlockSpec((128, CIN, EXT_W), lambda s: (1, 0, 0)),
            pl.BlockSpec((1, CIN, EXT_W), lambda s: (320, 0, 0)),
            vmem, vmem, vmem, vmem, vmem, vmem, vmem, vmem,
        ],
        out_specs=[vmem, vmem],
        out_shape=[
            jax.ShapeDtypeStruct((64, CORE_W, 128), F32),
            jax.ShapeDtypeStruct((2, CORE_W, 128), F32),
        ],
        scratch_shapes=[
            pltpu.VMEM((258 * TAPS, 256), BF16),
            pltpu.VMEM((2, 256, 128), F32),
            pltpu.VMEM((4 * TAPS, 256), BF16),
            pltpu.VMEM((4 * COUT, 256), BF16),
        ],
        compiler_params=pltpu.CompilerParams(vmem_limit_bytes=56 << 20),
        cost_estimate=pl.CostEstimate(flops=16 << 30, bytes_accessed=12 << 20, transcendentals=0),
    )(where, tissue, features, core, core, features, mleft, mright, left, right, *weights)


def finish_kernel(
    where_ref, rays_ref, prob_ref, edge_ref, above_ref, below_ref,
    out_ref, probability_ref, wide_ref, west_ref, east_ref, group_ref,
):
    tile_row = where_ref[0]
    quarter = lax.div(lanes_of((32, 128)), RAYS)

    def group(g, carry):
        rays = rays_ref[g]
        group_ref[...] = rays

        @pl.when(g < 16)
        def _():
            start = pl.multiple_of(g * 128, 128)
            group_ref[...] += above_ref[pl.ds(start, 128), :].astype(F32)

        @pl.when(g >= 48)
        def _():
            start = pl.multiple_of((g - 48) * 128, 128)
            group_ref[...] += below_ref[pl.ds(start, 128), :].astype(F32)

        phases = [group_ref[pl.ds(b, 32, stride=4), :] for b in range(4)]
        for p in range(4):
            row = phases[0] if p == 0 else pltpu.roll(phases[0], (-p * RAYS) % 128, 1)
            for b in range(1, 4):
                moved = phases[b] if b == p else pltpu.roll(phases[b], ((b - p) * RAYS) % 128, 1)
                row = jnp.where(quarter == b, moved, row)
            start = lax.div(g, 2) * 256 + lax.rem(g, 2) * 4 + p
            out_ref[pl.ds(start, 32, stride=8), :] = row
        return carry

    lax.fori_loop(0, 64, group, 0)
    lane = lanes_of((CORE_W, 128))
    above = above_ref[2048:2176, :].astype(F32) + above_ref[2176:2304, :].astype(F32)
    below = below_ref[2048:2176, :].astype(F32) + below_ref[2176:2304, :].astype(F32)
    first = prob_ref[0] + jnp.where(lane < 64, pltpu.roll(above, 120, 1), 0.0)
    last = prob_ref[1] + jnp.where(lane >= 64, pltpu.roll(below, 64, 1), 0.0)
    probability_ref[0:128, :] = first.T
    probability_ref[128:256, :] = last.T
    head = pltpu.roll(above, 122, 1) + pltpu.roll(edge_ref[0], 66, 1)
    head = jnp.where(tile_row > 0, head, 0.0)
    tail = pltpu.roll(edge_ref[1], 122, 1) + pltpu.roll(below, 66, 1)
    tail = jnp.where(tile_row < N_ROWS - 1, tail, 0.0)
    first_moved, last_moved = pltpu.roll(first, 2, 1), pltpu.roll(last, 2, 1)
    parts = [
        jnp.where(lane < 2, head, first_moved),
        jnp.where(lane < 2, first_moved, last_moved),
        jnp.where(lane < 2, last_moved, jnp.where(lane < 4, tail, 0.0)),
    ]
    for k, part in enumerate(parts):
        wide_ref[:, 128 * k : 128 * (k + 1)] = part
        west_ref[:, 128 * k : 128 * (k + 1)] = part[0:8]
        east_ref[:, 128 * k : 128 * (k + 1)] = part[120:128]


def finish(where, rays, prob, edge, above, below):
    smem = pl.BlockSpec(memory_space=pltpu.SMEM)
    vmem = pl.BlockSpec(memory_space=pltpu.VMEM)
    return pl.pallas_call(
        finish_kernel,
        in_specs=[smem, vmem, vmem, vmem, vmem, vmem],
        out_specs=[vmem] * 5,
        out_shape=[
            jax.ShapeDtypeStruct((8192, 128), F32),
            jax.ShapeDtypeStruct((CORE_H, CORE_W), F32),
            jax.ShapeDtypeStruct((CORE_W, 384), F32),
            jax.ShapeDtypeStruct((8, 384), F32),
            jax.ShapeDtypeStruct((8, 384), F32),
        ],
        scratch_shapes=[pltpu.VMEM((CORE_W, 128), F32)],
        compiler_params=pltpu.CompilerParams(vmem_limit_bytes=40 << 20),
        cost_estimate=pl.CostEstimate(flops=0, bytes_accessed=10 << 20, transcendentals=0),
    )(where, rays, prob, edge, above, below)


def peak_kernel(wide_ref, west_ref, east_ref, gap_ref, tall_ref):
    tall_ref[0:8, :] = west_ref[...]
    tall_ref[8:136, :] = wide_ref[...]
    tall_ref[136:144, :] = east_ref[...]
    best = tall_ref[6:134, :]
    for k in range(1, 5):
        best = jnp.maximum(best, tall_ref[6 + k : 134 + k, :])
    along = best
    for k in range(1, 5):
        along = jnp.maximum(along, pltpu.roll(best, 384 - k, 1))
    gap = along - pltpu.roll(wide_ref[...], 382, 1)
    gap_ref[0:128, :] = gap[:, 0:128].T
    gap_ref[128:256, :] = gap[:, 128:256].T


def peak(wide, west, east):
    vmem = pl.BlockSpec(memory_space=pltpu.VMEM)
    return pl.pallas_call(
        peak_kernel,
        in_specs=[vmem] * 3,
        out_specs=vmem,
        out_shape=jax.ShapeDtypeStruct((CORE_H, CORE_W), F32),
        scratch_shapes=[pltpu.VMEM((144, 384), F32)],
    )(wide, west, east)


def shift(array, axis, step):
    count = lax.axis_size(axis)
    pairs = [(i, i + step) for i in range(count) if 0 <= i + step < count]
    return lax.ppermute(array, axis, pairs)


def body(features, conv_weight, conv_bias, head_weight, head_bias, tissue):
    features = jnp.transpose(features, (0, 2, 1))
    where = jnp.stack([lax.axis_index("rows"), lax.axis_index("cols")]).astype(jnp.int32)
    hbias = jnp.pad(head_bias[None, :], ((0, 7), (0, 128 - head_bias.shape[0])))
    weights = (
        conv_weight.reshape(9 * CIN, COUT), conv_bias[None, :], jnp.transpose(head_weight), hbias,
    )
    to_right, to_left = pack_margin(tissue, features)
    mleft = shift(to_right, "cols", 1)
    mright = shift(to_left, "cols", -1)
    to_right, to_left = pack_core(features)
    cleft = shift(to_right, "cols", 1)
    cright = shift(to_left, "cols", -1)
    up, down, edge = margin_outputs(where, tissue, features, mleft, mright, weights)
    above = shift(down, "rows", 1)
    below = shift(up, "rows", -1)
    rays, prob = core_outputs(where, tissue, features, mleft, mright, cleft, cright, weights)
    out, probability, wide, west, east = finish(where, rays, prob, edge, above, below)
    from_west = shift(east, "cols", 1)
    from_east = shift(west, "cols", -1)
    gap = peak(wide, from_west, from_east)
    lengths = out.reshape(32, 32, 8, 128).transpose(0, 2, 1, 3).reshape(CORE_H, CORE_W * RAYS)
    return (probability, lengths, gap)


def solution(mesh):
    in_specs = (P("rows", "cols", None), P(), P(), P(), P(), P("rows", "cols"))
    out_specs = (P("rows", "cols"), P("rows", "cols"), P("rows", "cols"))
    return jax.shard_map(body, mesh=mesh, in_specs=in_specs, out_specs=out_specs, check_vma=False)
```

```python
import functools

import jax
import jax.numpy as jnp
from jax import lax
from jax.experimental import pallas as pl
from jax.experimental.pallas import tpu as pltpu
from jax.sharding import PartitionSpec as P

MARGIN = 64
EXT_H, EXT_W = 384, 256
CORE_H, CORE_W = 256, 128
N_ROWS, N_COLS = 8, 16
CIN, COUT, RAYS = 32, 128, 32
M_PAIRS = 74
C_PAIRS = 130
CHUNK = 8
SPAN = CHUNK + 2
M_CHUNKS = 9
C_CHUNKS = 16
M_OUT = M_CHUNKS * CHUNK
TAPS = 3 * CIN
F32, BF16 = jnp.float32, jnp.bfloat16


def lanes_of(shape):
    return lax.broadcasted_iota(jnp.int32, shape, len(shape) - 1)


def gauss(position, extent):
    spread = extent / 4.0
    centred = position.astype(F32) - (extent - 1) / 2.0
    return jnp.exp(-(centred * centred) / (2.0 * spread * spread))


def pack_pair(lo, hi, slot, right_ref, left_ref, extras):
    low_half = lanes_of((CIN, 128)) < 64
    place = lax.rem(slot, 128)
    spot = lanes_of((CIN, 128)) == place
    west_lo, east_lo = lo[:, :128], lo[:, 128:]
    west_hi, east_hi = hi[:, :128], hi[:, 128:]
    right_ref[slot] = jnp.where(low_half, pltpu.roll(east_lo, 64, 1), east_hi)
    left_ref[slot] = jnp.where(low_half, west_hi, pltpu.roll(west_lo, 64, 1))
    to_east = lax.rem(place + 128 - 63, 128)
    to_west = lax.rem(place + 128 - 64, 128)
    return (
        jnp.where(spot, pltpu.roll(east_lo, to_east, 1), extras[0]),
        jnp.where(spot, pltpu.roll(east_hi, to_east, 1), extras[1]),
        jnp.where(spot, pltpu.roll(west_lo, to_west, 1), extras[2]),
        jnp.where(spot, pltpu.roll(west_hi, to_west, 1), extras[3]),
    )


def pack_margin_kernel(tissue_ref, top_ref, bottom_ref, right_ref, left_ref):
    zero = jnp.zeros((CIN, 128), BF16)
    right_ref[0] = zero
    left_ref[0] = zero

    def step(t, extras):
        return pack_pair(top_ref[t], bottom_ref[95 - t], t + 1, right_ref, left_ref, extras)

    extras = lax.fori_loop(0, M_PAIRS - 2, step, (zero,) * 4, unroll=8)
    extras = step(M_PAIRS - 2, extras)
    flag = jnp.where(tissue_ref[0, 0] > 0, 1.0, 0.0)
    flags = jnp.full((CIN, 128), flag, F32).astype(BF16)
    for ref, lo, hi in ((right_ref, extras[0], extras[1]), (left_ref, extras[2], extras[3])):
        ref[M_PAIRS] = lo
        ref[M_PAIRS + 1] = hi
        ref[M_PAIRS + 2] = flags


def pack_margin(tissue, features):
    shape = jax.ShapeDtypeStruct((M_PAIRS + 3, CIN, 128), BF16)
    return pl.pallas_call(
        pack_margin_kernel,
        grid=(1,),
        in_specs=[
            pl.BlockSpec(memory_space=pltpu.SMEM),
            pl.BlockSpec((96, CIN, EXT_W), lambda s: (0, 0, 0)),
            pl.BlockSpec((96, CIN, EXT_W), lambda s: (3, 0, 0)),
        ],
        out_specs=[pl.BlockSpec(shape.shape, lambda s: (0, 0, 0))] * 2,
        out_shape=[shape, shape],
        compiler_params=pltpu.CompilerParams(vmem_limit_bytes=60 << 20),
        cost_estimate=pl.CostEstimate(flops=0, bytes_accessed=5 << 20, transcendentals=0),
    )(tissue, features, features)


def pack_core_kernel(features_ref, right_ref, left_ref):
    zero = jnp.zeros((CIN, 128), BF16)

    def step(slot, extras):
        return pack_pair(
            features_ref[MARGIN - 1 + slot], features_ref[EXT_H - MARGIN - slot], slot,
            right_ref, left_ref, extras,
        )

    extras = lax.fori_loop(0, 128, step, (zero,) * 4, unroll=8)
    more = lax.fori_loop(128, C_PAIRS, step, (zero,) * 4, unroll=2)
    for ref, k in ((right_ref, 0), (left_ref, 2)):
        ref[C_PAIRS] = extras[k]
        ref[C_PAIRS + 1] = more[k]
        ref[C_PAIRS + 2] = extras[k + 1]
        ref[C_PAIRS + 3] = more[k + 1]


def pack_core(features):
    shape = jax.ShapeDtypeStruct((C_PAIRS + 4, CIN, 128), BF16)
    vmem = pl.BlockSpec(memory_space=pltpu.VMEM)
    return pl.pallas_call(
        pack_core_kernel,
        in_specs=[vmem],
        out_specs=[vmem, vmem],
        out_shape=[shape, shape],
        compiler_params=pltpu.CompilerParams(vmem_limit_bytes=32 << 20),
        cost_estimate=pl.CostEstimate(flops=0, bytes_accessed=6 << 20, transcendentals=0),
    )(features)


def column_taps(own, strip, from_west, from_east):
    lane = lanes_of((CIN, 128))
    west, east = own[:, :128], own[:, 128:]
    zero = jnp.zeros((CIN, 128), BF16)

    def own_tap(shift):
        amount = 64 - shift
        return jnp.where(lane < amount, pltpu.roll(west, amount, 1), pltpu.roll(east, amount, 1))

    strip_minus = jnp.where(
        lane == 0, from_west, jnp.where(lane == 64, zero, pltpu.roll(strip, 1, 1))
    )
    strip_plus = jnp.where(
        lane == 127, from_east, jnp.where(lane == 63, zero, pltpu.roll(strip, 127, 1))
    )
    return (
        jnp.concatenate([own_tap(-1), strip_minus], axis=1),
        jnp.concatenate([own_tap(0), strip], axis=1),
        jnp.concatenate([own_tap(1), strip_plus], axis=1),
    )


def build_pair(own_lo, own_hi, left, right, extras, slot, lo_ref, hi_ref, place):
    low_half = lanes_of((CIN, 128)) < 64
    strip_lo = jnp.where(low_half, left, right)
    strip_hi = pltpu.roll(jnp.where(low_half, right, left), 64, 1)
    lane = lax.rem(slot, 128)
    to_first = lax.rem(128 - lane, 128)
    to_last = 127 - lane
    for own, strip, west, east, ref, row in (
        (own_lo, strip_lo, extras[0], extras[2], lo_ref, place),
        (own_hi, strip_hi, extras[1], extras[3], hi_ref, SPAN - 1 - place),
    ):
        parts = column_taps(own, strip, pltpu.roll(west, to_first, 1), pltpu.roll(east, to_last, 1))
        for k, part in enumerate(parts):
            ref[row * TAPS + k * CIN : row * TAPS + (k + 1) * CIN, :] = part


def build_chunk(chunk, first, pair, lo_ref, hi_ref):
    for place in range(first, SPAN):
        slot = chunk * CHUNK + place
        own_lo, own_hi, left, right, extras = pair(slot)
        build_pair(own_lo, own_hi, left, right, extras, slot, lo_ref, hi_ref, place)


def next_chunk(chunk, pair, lo_ref, hi_ref, next_lo_ref, next_hi_ref):
    next_lo_ref[0 : 2 * TAPS, :] = lo_ref[CHUNK * TAPS :, :]
    next_hi_ref[CHUNK * TAPS :, :] = hi_ref[0 : 2 * TAPS, :]
    build_chunk(chunk + 1, 2, pair, next_lo_ref, next_hi_ref)


def chunk_logits(lo_ref, hi_ref, conv_scr, head_scr, bias):
    return [
        [group_logits(ref, 4 * u, conv_scr, head_scr, bias) for u in range(2)]
        for ref in (lo_ref, hi_ref)
    ]


def walk(chunks, pair, refs, use):
    even, odd = refs[0:2], refs[2:4]

    def two(i, carry):
        use(2 * i, *even)
        next_chunk(2 * i, pair, *even, *odd)
        use(2 * i + 1, *odd)
        next_chunk(2 * i + 1, pair, *odd, *even)
        return carry

    if chunks > 2:
        lax.fori_loop(0, (chunks - 1) // 2, two, 0)
    last = chunks - 1
    if chunks % 2:
        use(last, *even)
    else:
        use(last - 1, *even)
        next_chunk(last - 1, pair, *even, *odd)
        use(last, *odd)


def prepare_weights(conv_ref, head_ref, bias_ref, conv_scr, head_scr):
    zero = jnp.zeros((TAPS, COUT), BF16)
    conv_scr[0 : 3 * TAPS, 0:COUT] = conv_ref[...]
    conv_scr[3 * TAPS : 4 * TAPS, 0:COUT] = zero
    conv_scr[0:TAPS, COUT:] = zero
    conv_scr[TAPS : 4 * TAPS, COUT:] = conv_ref[...]
    head = head_ref[...].astype(F32)
    head = jnp.concatenate([head, jnp.zeros((COUT - head.shape[0], COUT), F32)], axis=0).T
    lane = lanes_of((COUT, 128))
    for r in range(4):
        rays = pltpu.roll(head, (r * RAYS - 1) % 128, 1)
        rays = jnp.where((lane >= r * RAYS) & (lane < (r + 1) * RAYS), rays, 0.0)
        prob = jnp.where(lane == r, pltpu.roll(head, r, 1), 0.0)
        head_scr[r * COUT : (r + 1) * COUT, 0:128] = rays.astype(BF16)
        head_scr[r * COUT : (r + 1) * COUT, 128:256] = prob.astype(BF16)


def spread_bias(head_bias):
    lane = lanes_of((8, 128))
    rays = jnp.zeros((8, 128), F32)
    for r in range(4):
        moved = pltpu.roll(head_bias, (r * RAYS - 1) % 128, 1)
        rays = jnp.where((lane >= r * RAYS) & (lane < (r + 1) * RAYS), moved, rays)
    return rays[0:1]


def column_weights(tile_col, tissue, left_flags, right_flags):
    q = lax.broadcasted_iota(jnp.int32, (CORE_W, 128), 0)
    own = gauss(q + MARGIN, EXT_W)
    west = gauss(q + CORE_W + MARGIN, EXT_W)
    east = gauss(q - MARGIN, EXT_W)
    west_side = q < MARGIN
    has_west = jnp.where(tile_col > 0, 1.0, 0.0)
    has_east = jnp.where(tile_col < N_COLS - 1, 1.0, 0.0)
    side = jnp.where(west_side, west, east)
    total = own + side * jnp.where(west_side, has_west, has_east)
    flags = jnp.concatenate([left_flags, left_flags, right_flags, right_flags], axis=0)
    return own / total * jnp.where(tissue > 0, 1.0, 0.0), side / total * flags


def row_weights(row, tile_row):
    own = gauss(row, EXT_H)
    above = gauss(row + CORE_H, EXT_H) * jnp.where(tile_row > 0, 1.0, 0.0)
    below = gauss(row - CORE_H, EXT_H) * jnp.where(tile_row < N_ROWS - 1, 1.0, 0.0)
    total = own + jnp.where(row < 2 * MARGIN, above, 0.0) + jnp.where(row >= CORE_H, below, 0.0)
    return own / total


def group_logits(taps_ref, base, conv_scr, head_scr, bias):
    hidden = []
    for pair in range(2):
        start = (base + 2 * pair) * TAPS
        summed = lax.dot_general(
            taps_ref[start : start + 4 * TAPS, :],
            conv_scr[...],
            (((0,), (0,)), ((), ())),
            preferred_element_type=F32,
        )
        hidden.append(jnp.maximum(summed + bias, 0.0).astype(BF16))
    return jnp.dot(
        jnp.concatenate(hidden, axis=1), head_scr[...], preferred_element_type=F32
    )


def probability_block(logits, bias, first_row, tile_row, own_weight, side_weight):
    rows = lanes_of((CORE_W, 128)) + first_row
    values = 1.0 / (1.0 + jnp.exp(-(logits + bias)))
    return (values[:CORE_W] * own_weight + values[CORE_W:] * side_weight) * row_weights(
        rows, tile_row
    )


def weighted_rays(logits, ray_bias, own_weight, side_weight, first_row, tile_row):
    quarter = lax.div(lanes_of((1, 128)), RAYS)
    factor = row_weights(first_row + quarter, tile_row)
    return (
        (logits[:CORE_W, :128] + ray_bias) * own_weight
        + (logits[CORE_W:, :128] + ray_bias) * side_weight
    ) * factor


def add_probability(logit_ref, block, logits, first_lane):
    both = logits[0][:, 128:] + pltpu.roll(logits[1][:, 128:], 4, 1)
    logit_ref[block] += pltpu.roll(both, first_lane, 1)


def margin_kernel(
    where_ref, tissue_ref, top_ref, bottom_ref, left_ref, right_ref,
    conv_ref, bias_ref, head_ref, hbias_ref,
    up_ref, down_ref, edge_ref,
    lo0_ref, hi0_ref, lo1_ref, hi1_ref, logit_ref, conv_scr, head_scr,
):
    tile_row, tile_col = where_ref[0], where_ref[1]
    prepare_weights(conv_ref, head_ref, bias_ref, conv_scr, head_scr)
    extras = (left_ref[M_PAIRS], left_ref[M_PAIRS + 1], right_ref[M_PAIRS], right_ref[M_PAIRS + 1])

    def pair(slot):
        row = slot - 1 if isinstance(slot, jax.Array) else max(slot - 1, 0)
        return top_ref[row], bottom_ref[95 - row], left_ref[slot], right_ref[slot], extras

    build_chunk(0, 0, pair, lo0_ref, hi0_ref)
    lo0_ref[0:TAPS, :] = jnp.zeros((TAPS, 256), BF16)
    hi0_ref[(SPAN - 1) * TAPS :, :] = jnp.zeros((TAPS, 256), BF16)
    own_weight, side_weight = column_weights(
        tile_col, tissue_ref[0, 0],
        left_ref[M_PAIRS + 2].astype(F32), right_ref[M_PAIRS + 2].astype(F32),
    )
    bias = jnp.concatenate([bias_ref[...], bias_ref[...]], axis=1)
    ray_bias = spread_bias(hbias_ref[...])
    logit_ref[...] = jnp.zeros(logit_ref.shape, F32)

    def use(chunk, lo_ref, hi_ref):
        lo, hi = chunk_logits(lo_ref, hi_ref, conv_scr, head_scr, bias)
        for u in range(2):
            start = pl.multiple_of((2 * chunk + u) * 128, 128)
            first_row = CHUNK * chunk + 4 * u
            up_ref[pl.ds(start, 128), :] = weighted_rays(
                lo[u], ray_bias, own_weight, side_weight, first_row, tile_row
            ).astype(BF16)
            first_row = EXT_H - CHUNK * (chunk + 1) + 4 * u
            group = 14 - 2 * chunk + u
            start = pl.multiple_of(jnp.where(group < 0, group + 18, group) * 128, 128)
            down_ref[pl.ds(start, 128), :] = weighted_rays(
                hi[u], ray_bias, own_weight, side_weight, first_row, tile_row
            ).astype(BF16)
        add_probability(logit_ref, 0, lo, CHUNK * chunk)
        add_probability(logit_ref, 1, hi, M_OUT - CHUNK * (chunk + 1))

    walk(M_CHUNKS, pair, (lo0_ref, hi0_ref, lo1_ref, hi1_ref), use)
    for block, first_row, ref in ((0, 0, up_ref), (1, EXT_H - M_OUT, down_ref)):
        prob = probability_block(
            logit_ref[block], hbias_ref[0, 0], first_row, tile_row, own_weight, side_weight
        )
        prob = jnp.where(lanes_of((CORE_W, 128)) < M_OUT, prob, 0.0)
        edge_ref[block] = prob
        high = prob.astype(BF16)
        ref[2048:2176, :] = high
        ref[2176:2304, :] = (prob - high.astype(F32)).astype(BF16)


def conv_scratch():
    return [pltpu.VMEM((SPAN * TAPS, 256), BF16)] * 4 + [
        pltpu.VMEM((2, 256, 128), F32),
        pltpu.VMEM((4 * TAPS, 256), BF16),
        pltpu.VMEM((4 * COUT, 256), BF16),
    ]


def margin_outputs(where, tissue, features, left, right, weights):
    shape = jax.ShapeDtypeStruct((2304, 128), BF16)
    edge = jax.ShapeDtypeStruct((2, CORE_W, 128), F32)
    smem = pl.BlockSpec(memory_space=pltpu.SMEM)
    vmem = pl.BlockSpec(memory_space=pltpu.VMEM)
    return pl.pallas_call(
        margin_kernel,
        grid=(1,),
        in_specs=[
            smem, smem,
            pl.BlockSpec((96, CIN, EXT_W), lambda s: (0, 0, 0)),
            pl.BlockSpec((96, CIN, EXT_W), lambda s: (3, 0, 0)),
            vmem, vmem, vmem, vmem, vmem, vmem,
        ],
        out_specs=[vmem, vmem, vmem],
        out_shape=[shape, shape, edge],
        scratch_shapes=conv_scratch(),
        compiler_params=pltpu.CompilerParams(vmem_limit_bytes=32 << 20),
        cost_estimate=pl.CostEstimate(flops=8 << 30, bytes_accessed=8 << 20, transcendentals=0),
    )(where, tissue, features, features, left, right, *weights)


def core_kernel(
    where_ref, tissue_ref, features_ref, mleft_ref, mright_ref, left_ref, right_ref,
    conv_ref, bias_ref, head_ref, hbias_ref,
    rays_ref, prob_ref,
    lo0_ref, hi0_ref, lo1_ref, hi1_ref, logit_ref, conv_scr, head_scr,
):
    tile_row, tile_col = where_ref[0], where_ref[1]
    prepare_weights(conv_ref, head_ref, bias_ref, conv_scr, head_scr)

    def pair(slot):
        block = C_PAIRS + slot // 128
        extras = (left_ref[block], left_ref[block + 2], right_ref[block], right_ref[block + 2])
        return (
            features_ref[MARGIN - 1 + slot], features_ref[EXT_H - MARGIN - slot],
            left_ref[slot], right_ref[slot], extras,
        )

    build_chunk(0, 0, pair, lo0_ref, hi0_ref)
    own_weight, side_weight = column_weights(
        tile_col, tissue_ref[0, 0], mleft_ref[0].astype(F32), mright_ref[0].astype(F32)
    )
    bias = jnp.concatenate([bias_ref[...], bias_ref[...]], axis=1)
    ray_bias = spread_bias(hbias_ref[...])
    logit_ref[...] = jnp.zeros(logit_ref.shape, F32)

    def use(chunk, lo_ref, hi_ref):
        lo, hi = chunk_logits(lo_ref, hi_ref, conv_scr, head_scr, bias)
        for u in range(2):
            group = 2 * chunk + u
            rays_ref[group] = weighted_rays(
                lo[u], ray_bias, own_weight, side_weight, MARGIN + 4 * group, tile_row
            )
            group = 62 - 2 * chunk + u
            rays_ref[group] = weighted_rays(
                hi[u], ray_bias, own_weight, side_weight, MARGIN + 4 * group, tile_row
            )
        add_probability(logit_ref, 0, lo, CHUNK * chunk)
        add_probability(logit_ref, 1, hi, 128 - CHUNK * (chunk + 1))

    walk(C_CHUNKS, pair, (lo0_ref, hi0_ref, lo1_ref, hi1_ref), use)
    for block in range(2):
        prob_ref[block] = probability_block(
            logit_ref[block], hbias_ref[0, 0], MARGIN + 128 * block, tile_row,
            own_weight, side_weight,
        )


def core_outputs(where, tissue, features, mleft, mright, left, right, weights):
    smem = pl.BlockSpec(memory_space=pltpu.SMEM)
    vmem = pl.BlockSpec(memory_space=pltpu.VMEM)
    flag = pl.BlockSpec((1, CIN, 128), lambda s: (M_PAIRS + 2, 0, 0))
    return pl.pallas_call(
        core_kernel,
        grid=(1,),
        in_specs=[smem, smem, vmem, flag, flag, vmem, vmem, vmem, vmem, vmem, vmem],
        out_specs=[vmem, vmem],
        out_shape=[
            jax.ShapeDtypeStruct((64, CORE_W, 128), F32),
            jax.ShapeDtypeStruct((2, CORE_W, 128), F32),
        ],
        scratch_shapes=conv_scratch(),
        compiler_params=pltpu.CompilerParams(vmem_limit_bytes=40 << 20),
        cost_estimate=pl.CostEstimate(flops=16 << 30, bytes_accessed=12 << 20, transcendentals=0),
    )(where, tissue, features, mleft, mright, left, right, *weights)


def finish_kernel(
    where_ref, rays_ref, prob_ref, edge_ref, above_ref, below_ref,
    out_ref, probability_ref, wide_ref, west_ref, east_ref, group_ref,
):
    tile_row = where_ref[0]
    quarter = lax.div(lanes_of((32, 128)), RAYS)

    def group(g, carry):
        rays = rays_ref[g]
        group_ref[...] = rays

        @pl.when(g < 16)
        def _():
            start = pl.multiple_of(g * 128, 128)
            group_ref[...] += above_ref[pl.ds(start, 128), :].astype(F32)

        @pl.when(g >= 48)
        def _():
            start = pl.multiple_of((g - 48) * 128, 128)
            group_ref[...] += below_ref[pl.ds(start, 128), :].astype(F32)

        phases = [group_ref[pl.ds(b, 32, stride=4), :] for b in range(4)]
        for p in range(4):
            row = phases[0] if p == 0 else pltpu.roll(phases[0], (-p * RAYS) % 128, 1)
            for b in range(1, 4):
                moved = phases[b] if b == p else pltpu.roll(phases[b], ((b - p) * RAYS) % 128, 1)
                row = jnp.where(quarter == b, moved, row)
            start = lax.div(g, 2) * 256 + lax.rem(g, 2) * 4 + p
            out_ref[pl.ds(start, 32, stride=8), :] = row
        return carry

    lax.fori_loop(0, 64, group, 0)
    lane = lanes_of((CORE_W, 128))
    above = above_ref[2048:2176, :].astype(F32) + above_ref[2176:2304, :].astype(F32)
    below = below_ref[2048:2176, :].astype(F32) + below_ref[2176:2304, :].astype(F32)
    first = prob_ref[0] + jnp.where(lane < 64, pltpu.roll(above, 120, 1), 0.0)
    last = prob_ref[1] + jnp.where(lane >= 64, pltpu.roll(below, 64, 1), 0.0)
    probability_ref[0:128, :] = first.T
    probability_ref[128:256, :] = last.T
    head = pltpu.roll(above, 122, 1) + pltpu.roll(edge_ref[0], 66, 1)
    head = jnp.where(tile_row > 0, head, 0.0)
    tail = pltpu.roll(edge_ref[1], 122, 1) + pltpu.roll(below, 66, 1)
    tail = jnp.where(tile_row < N_ROWS - 1, tail, 0.0)
    first_moved, last_moved = pltpu.roll(first, 2, 1), pltpu.roll(last, 2, 1)
    parts = [
        jnp.where(lane < 2, head, first_moved),
        jnp.where(lane < 2, first_moved, last_moved),
        jnp.where(lane < 2, last_moved, jnp.where(lane < 4, tail, 0.0)),
    ]
    for k, part in enumerate(parts):
        wide_ref[:, 128 * k : 128 * (k + 1)] = part
        west_ref[:, 128 * k : 128 * (k + 1)] = part[0:8]
        east_ref[:, 128 * k : 128 * (k + 1)] = part[120:128]


def finish(where, rays, prob, edge, above, below):
    smem = pl.BlockSpec(memory_space=pltpu.SMEM)
    vmem = pl.BlockSpec(memory_space=pltpu.VMEM)
    return pl.pallas_call(
        finish_kernel,
        in_specs=[smem, vmem, vmem, vmem, vmem, vmem],
        out_specs=[vmem] * 5,
        out_shape=[
            jax.ShapeDtypeStruct((8192, 128), F32),
            jax.ShapeDtypeStruct((CORE_H, CORE_W), F32),
            jax.ShapeDtypeStruct((CORE_W, 384), F32),
            jax.ShapeDtypeStruct((8, 384), F32),
            jax.ShapeDtypeStruct((8, 384), F32),
        ],
        scratch_shapes=[pltpu.VMEM((CORE_W, 128), F32)],
        compiler_params=pltpu.CompilerParams(vmem_limit_bytes=40 << 20),
        cost_estimate=pl.CostEstimate(flops=0, bytes_accessed=10 << 20, transcendentals=0),
    )(where, rays, prob, edge, above, below)


def peak_kernel(wide_ref, west_ref, east_ref, gap_ref, tall_ref):
    tall_ref[0:8, :] = west_ref[...]
    tall_ref[8:136, :] = wide_ref[...]
    tall_ref[136:144, :] = east_ref[...]
    best = tall_ref[6:134, :]
    for k in range(1, 5):
        best = jnp.maximum(best, tall_ref[6 + k : 134 + k, :])
    along = best
    for k in range(1, 5):
        along = jnp.maximum(along, pltpu.roll(best, 384 - k, 1))
    gap = along - pltpu.roll(wide_ref[...], 382, 1)
    gap_ref[0:128, :] = gap[:, 0:128].T
    gap_ref[128:256, :] = gap[:, 128:256].T


def peak(wide, west, east):
    vmem = pl.BlockSpec(memory_space=pltpu.VMEM)
    return pl.pallas_call(
        peak_kernel,
        in_specs=[vmem] * 3,
        out_specs=vmem,
        out_shape=jax.ShapeDtypeStruct((CORE_H, CORE_W), F32),
        scratch_shapes=[pltpu.VMEM((144, 384), F32)],
    )(wide, west, east)


def shift(array, axis, step):
    count = lax.axis_size(axis)
    pairs = [(i, i + step) for i in range(count) if 0 <= i + step < count]
    return lax.ppermute(array, axis, pairs)


def body(features, conv_weight, conv_bias, head_weight, head_bias, tissue):
    features = jnp.transpose(features, (0, 2, 1))
    where = jnp.stack([lax.axis_index("rows"), lax.axis_index("cols")]).astype(jnp.int32)
    hbias = jnp.pad(head_bias[None, :], ((0, 7), (0, 128 - head_bias.shape[0])))
    weights = (
        conv_weight.reshape(9 * CIN, COUT), conv_bias[None, :], jnp.transpose(head_weight), hbias,
    )
    to_right, to_left = pack_margin(tissue, features)
    mleft = shift(to_right, "cols", 1)
    mright = shift(to_left, "cols", -1)
    to_right, to_left = pack_core(features)
    cleft = shift(to_right, "cols", 1)
    cright = shift(to_left, "cols", -1)
    up, down, edge = margin_outputs(where, tissue, features, mleft, mright, weights)
    above = shift(down, "rows", 1)
    below = shift(up, "rows", -1)
    rays, prob = core_outputs(where, tissue, features, mleft, mright, cleft, cright, weights)
    out, probability, wide, west, east = finish(where, rays, prob, edge, above, below)
    from_west = shift(east, "cols", 1)
    from_east = shift(west, "cols", -1)
    gap = peak(wide, from_west, from_east)
    lengths = out.reshape(32, 32, 8, 128).transpose(0, 2, 1, 3).reshape(CORE_H, CORE_W * RAYS)
    return (probability, lengths, gap)


def solution(mesh):
    in_specs = (P("rows", "cols", None), P(), P(), P(), P(), P("rows", "cols"))
    out_specs = (P("rows", "cols"), P("rows", "cols"), P("rows", "cols"))
    return jax.shard_map(body, mesh=mesh, in_specs=in_specs, out_specs=out_specs, check_vma=False)
```

```python
import jax
import jax.numpy as jnp
from jax import lax
from jax.experimental import pallas as pl
from jax.experimental.pallas import tpu as pltpu
from jax.sharding import PartitionSpec as P

MARGIN = 64
EXT_H, EXT_W = 384, 256
CORE_H, CORE_W = 256, 128
N_ROWS, N_COLS = 8, 16
CIN, COUT, RAYS = 32, 128, 32
SIDE = 80
M_HALF = 19
M_BLOCKS = 2 * M_HALF
C_FIRST = 16
C_BLOCKS = 65
M_GROUPS = 18
M_OUT = 4 * M_GROUPS
GAP = 88
F32, BF16 = jnp.float32, jnp.bfloat16
SMEM = pl.BlockSpec(memory_space=pltpu.SMEM)
VMEM = pl.BlockSpec(memory_space=pltpu.VMEM)


def lanes_of(shape):
    return lax.broadcasted_iota(jnp.int32, shape, len(shape) - 1)


def gauss(position, extent):
    spread = extent / 4.0
    centred = position.astype(F32) - (extent - 1) / 2.0
    return jnp.exp(-(centred * centred) / (2.0 * spread * spread))


def turn(rows, index, right_ref, left_ref):
    block = jnp.concatenate(rows, axis=0).T
    right_ref[index] = block[EXT_W - SIDE :]
    left_ref[index] = block[:SIDE]


def turn_margin_kernel(tissue_ref, top_ref, bottom_ref, right_ref, left_ref):
    zero = jnp.zeros((CIN, EXT_W), BF16)
    turn([zero] + [top_ref[k] for k in range(3)], 0, right_ref, left_ref)
    turn([bottom_ref[95], zero, zero, zero], M_BLOCKS - 1, right_ref, left_ref)

    def step(m, carry):
        rows = [top_ref[4 * m - 1 + k] for k in range(4)]
        turn(rows, m, right_ref, left_ref)
        rows = [bottom_ref[19 + 4 * m + k] for k in range(4)]
        turn(rows, M_HALF - 1 + m, right_ref, left_ref)
        return carry

    lax.fori_loop(1, M_HALF, step, 0, unroll=6)
    flag = jnp.where(tissue_ref[0, 0] > 0, 1.0, 0.0)
    flags = jnp.full((SIDE, 128), flag, F32).astype(BF16)
    right_ref[M_BLOCKS] = flags
    left_ref[M_BLOCKS] = flags


def turn_margin(tissue, features):
    side = jax.ShapeDtypeStruct((M_BLOCKS + 1, SIDE, 128), BF16)
    return pl.pallas_call(
        turn_margin_kernel,
        grid=(1,),
        in_specs=[
            SMEM,
            pl.BlockSpec((96, CIN, EXT_W), lambda s: (0, 0, 0)),
            pl.BlockSpec((96, CIN, EXT_W), lambda s: (3, 0, 0)),
        ],
        out_specs=[VMEM, VMEM],
        out_shape=[side, side],
        compiler_params=pltpu.CompilerParams(vmem_limit_bytes=60 << 20),
        cost_estimate=pl.CostEstimate(flops=0, bytes_accessed=8 << 20, transcendentals=0),
    )(tissue, features, features)


def turn_core_kernel(features_ref, right_ref, left_ref):
    def step(m, carry):
        rows = [features_ref[4 * (C_FIRST + m) - 1 + k] for k in range(4)]
        turn(rows, m, right_ref, left_ref)
        return carry

    lax.fori_loop(0, C_BLOCKS, step, 0, unroll=13)


def turn_core(features):
    side = jax.ShapeDtypeStruct((C_BLOCKS, SIDE, 128), BF16)
    return pl.pallas_call(
        turn_core_kernel,
        in_specs=[VMEM],
        out_specs=[VMEM, VMEM],
        out_shape=[side, side],
        compiler_params=pltpu.CompilerParams(vmem_limit_bytes=60 << 20),
        cost_estimate=pl.CostEstimate(flops=0, bytes_accessed=12 << 20, transcendentals=0),
    )(features)


def prepare_weights(conv_ref, head_ref, conv_scr, head_scr):
    zero = jnp.zeros((CIN, COUT), BF16)
    for o in range(2):
        for i in range(4):
            for dc in range(3):
                dr = i - o
                piece = zero
                if 0 <= dr < 3:
                    piece = conv_ref[(3 * dr + dc) * CIN : (3 * dr + dc + 1) * CIN, :]
                row = dc * 128 + i * CIN
                conv_scr[row : row + CIN, o * COUT : (o + 1) * COUT] = piece
    head = head_ref[...].astype(F32)
    head = jnp.concatenate([head, jnp.zeros((COUT - head.shape[0], COUT), F32)], axis=0).T
    part = lax.div(lanes_of((COUT, 128)), RAYS)
    first = jnp.broadcast_to(head[:, 0:1], (COUT, 128))
    for b in range(4):
        rays = jnp.where(part == b, pltpu.roll(head, (b * RAYS - 1) % 128, 1), 0.0)
        prob = jnp.where(part == b, first, 0.0)
        head_scr[b * COUT : (b + 1) * COUT, 0:128] = rays.astype(BF16)
        head_scr[b * COUT : (b + 1) * COUT, 128:256] = prob.astype(BF16)


def spread_bias(head_bias):
    part = lax.div(lanes_of((8, 128)), RAYS)
    rays = jnp.zeros((8, 128), F32)
    for b in range(4):
        rays = jnp.where(part == b, pltpu.roll(head_bias, (b * RAYS - 1) % 128, 1), rays)
    return rays[0:1]


def column_weights(tile_col, tissue, left_flags, right_flags):
    q = lax.broadcasted_iota(jnp.int32, (32, 128), 0) * 4 + lax.div(lanes_of((32, 128)), RAYS)
    own = gauss(q + MARGIN, EXT_W)
    west_side = q < MARGIN
    side = jnp.where(west_side, gauss(q + CORE_W + MARGIN, EXT_W), gauss(q - MARGIN, EXT_W))
    has_west = jnp.where(tile_col > 0, 1.0, 0.0)
    has_east = jnp.where(tile_col < N_COLS - 1, 1.0, 0.0)
    total = own + side * jnp.where(west_side, has_west, has_east)
    flags = jnp.concatenate([left_flags[:16], right_flags[:16]], axis=0)
    return own / total * jnp.where(tissue > 0, 1.0, 0.0), side / total * flags


def row_weights(row, tile_row):
    own = gauss(row, EXT_H)
    above = gauss(row + CORE_H, EXT_H) * jnp.where(tile_row > 0, 1.0, 0.0)
    below = gauss(row - CORE_H, EXT_H) * jnp.where(tile_row < N_ROWS - 1, 1.0, 0.0)
    total = own + jnp.where(row < 2 * MARGIN, above, 0.0) + jnp.where(row >= CORE_H, below, 0.0)
    return own / total


def slid(now, later):
    low_half = lanes_of(now.shape) < 64
    return pltpu.roll(jnp.where(low_half, later, now), 64, 1)


def window_taps(own, left, right, own_f, side_f, taps_ref, w):
    own_f[...] = own.astype(F32)
    side_f[0:SIDE, :] = left.astype(F32)
    side_f[GAP : GAP + SIDE, :] = right.astype(F32)
    for d in range(3):
        lanes = slice(128 * d, 128 * (d + 1))
        for b in range(4):
            row = 256 * w + 32 * b
            taps_ref[row : row + 32, lanes] = own_f[pl.ds(15 + b + d, 32, stride=4), :].astype(BF16)
            west = side_f[pl.ds(15 + b + d, 16, stride=4), :]
            east = side_f[pl.ds(GAP - 1 + b + d, 16, stride=4), :]
            taps_ref[row + 128 : row + 144, lanes] = west.astype(BF16)
            taps_ref[row + 144 : row + 160, lanes] = east.astype(BF16)


def turned(rows):
    return jnp.concatenate(rows, axis=0).T[48:208]


def groups_taps(sources, buffers, taps_ref):
    for k, (now, later) in enumerate(sources):
        windows = now, tuple(slid(x, y) for x, y in zip(now, later))
        for w, window in enumerate(windows):
            at = 2 * k + w
            window_taps(*window, buffers[2 * at], buffers[2 * at + 1], taps_ref, at)


def groups_hidden(taps_ref, hidden_ref, conv_scr, bias):
    for first in range(0, taps_ref.shape[0], CONV_CHUNK):
        summed = jnp.dot(
            taps_ref[first : first + CONV_CHUNK, :], conv_scr[...], preferred_element_type=F32
        )
        hidden = jnp.maximum(summed + bias, 0.0).astype(BF16)
        for w in range(CONV_CHUNK // 256):
            for o in range(2):
                for s in range(2):
                    row = first // 2 + 32 * (4 * w + 2 * o + s)
                    for b in range(4):
                        start = 256 * w + 128 * s + 32 * b
                        hidden_ref[row : row + 32, b * COUT : (b + 1) * COUT] = hidden[
                            start : start + 32, o * COUT : (o + 1) * COUT
                        ]


def head_logits(hidden_ref, head_scr):
    every = []
    for first in range(0, hidden_ref.shape[0], HEAD_CHUNK):
        logits = jnp.dot(
            hidden_ref[first : first + HEAD_CHUNK, :], head_scr[...], preferred_element_type=F32
        )
        every += [logits[k : k + 256] for k in range(0, HEAD_CHUNK, 256)]
    return every


def walk(count, taps_stage, hidden_stage, head_stage, taps, hidden):
    taps_stage(0, taps[0])
    taps_stage(1, taps[1])
    hidden_stage(taps[0], hidden[0])

    def two(n, carry):
        for odd in (1, 0):
            i = 2 * n + 2 - odd
            taps_stage(i + 1, taps[1 - odd])
            hidden_stage(taps[odd], hidden[odd])
            head_stage(i - 1, hidden[1 - odd])
        return carry

    lax.fori_loop(0, (count - 2) // 2, two, 0)
    head_stage(count - 2, hidden[0])
    hidden_stage(taps[1], hidden[1])
    head_stage(count - 1, hidden[1])


def split_logits(logits, r):
    return logits[64 * r : 64 * r + 32], logits[64 * r + 32 : 64 * r + 64]


def weighted_rays(logits, r, ray_bias, own_weight, side_weight, row, factor_ref):
    own, side = split_logits(logits, r)
    factor = factor_ref[pl.ds(row, 1), :]
    return (
        (own[:, :128] + ray_bias) * own_weight + (side[:, :128] + ray_bias) * side_weight
    ) * factor


def keep_probability(logit_ref, logits, r, position):
    spot = lax.rem(lanes_of((32, 128)), RAYS) == lax.rem(position, RAYS)
    block = lax.div(position, RAYS)
    for k, part in enumerate(split_logits(logits, r)):
        logit_ref[k, block] = jnp.where(spot, part[:, 128:], logit_ref[k, block])


def probability_by_row(logit_ref, first_block, blocks, first_row, bias, tile_row, own_weight, side_weight, out_ref):
    lane = lanes_of((32, 128))
    values = []
    for j in range(blocks):
        own = 1.0 / (1.0 + jnp.exp(-(logit_ref[0, first_block + j] + bias)))
        side = 1.0 / (1.0 + jnp.exp(-(logit_ref[1, first_block + j] + bias)))
        factor = row_weights(first_row + 32 * j + lax.rem(lane, RAYS), tile_row)
        values.append((own * own_weight + side * side_weight) * factor)
    for b in range(4):
        rows = jnp.zeros((32, 128), F32)
        for j in range(blocks):
            moved = values[j] if j == b else pltpu.roll(values[j], ((j - b) * 32) % 128, 1)
            rows = jnp.where(lax.div(lane, 32) == j, moved, rows)
        out_ref[pl.ds(b, 32, stride=4), :] = rows


def margin_kernel(
    where_ref, tissue_ref, features_ref, left_ref, right_ref, conv_ref, bias_ref, head_ref, hbias_ref,
    up_ref, down_ref, edge_ref,
    logit_ref, turn_ref, factor_ref, conv_scr, head_scr, taps0, taps1, hidden0, hidden1, *buffers,
):
    tile_row, tile_col = where_ref[0], where_ref[1]
    prepare_weights(conv_ref, head_ref, conv_scr, head_scr)
    for k in range(len(buffers) // 2):
        buffers[2 * k + 1][SIDE:GAP, :] = jnp.zeros((GAP - SIDE, 128), F32)
    own_weight, side_weight = column_weights(
        tile_col, tissue_ref[0, 0], left_ref[M_BLOCKS].astype(F32), right_ref[M_BLOCKS].astype(F32)
    )
    bias = jnp.concatenate([bias_ref[...], bias_ref[...]], axis=1)
    ray_bias = spread_bias(hbias_ref[...])
    logit_ref[...] = jnp.zeros(logit_ref.shape, F32)
    table = lax.broadcasted_iota(jnp.int32, (EXT_H, 128), 0)
    factor_ref[...] = row_weights(table, tile_row)

    def taps_stage(g, taps_ref):
        def source(first_block, first_row, block):
            rows = []
            for k in range(4):
                row = first_row + 4 * block - 1 + k
                inside = (row >= 0) & (row < EXT_H)
                values = features_ref[jnp.where(inside, row, 0)]
                rows.append(jnp.where(inside, values, jnp.zeros_like(values)))
            at = first_block + block
            return turned(rows), left_ref[at], right_ref[at]

        groups_taps(
            [
                (source(*half, g), source(*half, g + 1))
                for half in ((0, 0), (M_HALF, EXT_H - M_OUT))
            ],
            buffers, taps_ref,
        )

    def hidden_stage(taps_ref, hidden_ref):
        groups_hidden(taps_ref, hidden_ref, conv_scr, bias)

    def head_stage(g, hidden_ref):
        every = head_logits(hidden_ref, head_scr)
        for half, (ref, first_row) in enumerate(((up_ref, 0), (down_ref, EXT_H - M_OUT))):
            logits = every[half]
            for r in range(4):
                position = 4 * g + r
                rays = weighted_rays(
                    logits, r, ray_bias, own_weight, side_weight, first_row + position, factor_ref
                )
                slot = position
                if half == 1:
                    slot = jnp.where(position < 8, position + 64, position - 8)
                ref[pl.ds(pl.multiple_of(slot * 32, 32), 32), :] = rays.astype(BF16)
                keep_probability(logit_ref, logits, r, position + 96 * half)

    walk(M_GROUPS, taps_stage, hidden_stage, head_stage, (taps0, taps1), (hidden0, hidden1))
    for half, (ref, first_row) in enumerate(((up_ref, 0), (down_ref, EXT_H - M_OUT))):
        probability_by_row(
            logit_ref, 3 * half, 3, first_row, hbias_ref[0, 0], tile_row,
            own_weight, side_weight, turn_ref,
        )
        prob = jnp.where(lanes_of((CORE_W, 128)) < M_OUT, turn_ref[...], 0.0)
        edge_ref[half] = prob
        high = prob.astype(BF16)
        ref[2048:2176, :] = high
        ref[2176:2304, :] = (prob - high.astype(F32)).astype(BF16)


C_GROUPS = 4
CONV_CHUNK, HEAD_CHUNK = 256, 256


def conv_scratch(groups, logit_blocks):
    return [
        pltpu.VMEM((2, logit_blocks, 32, 128), F32),
        pltpu.VMEM((CORE_W, 128), F32),
        pltpu.VMEM((EXT_H, 128), F32),
        pltpu.VMEM((384, 256), BF16),
        pltpu.VMEM((4 * COUT, 256), BF16),
        pltpu.VMEM((512 * groups, 384), BF16),
        pltpu.VMEM((512 * groups, 384), BF16),
        pltpu.VMEM((256 * groups, 512), BF16),
        pltpu.VMEM((256 * groups, 512), BF16),
    ] + [pltpu.VMEM((160, 128), F32), pltpu.VMEM((GAP + SIDE, 128), F32)] * (2 * groups)


def margin_outputs(where, tissue, features, left, right, weights):
    shape = jax.ShapeDtypeStruct((2304, 128), BF16)
    edge = jax.ShapeDtypeStruct((2, CORE_W, 128), F32)
    return pl.pallas_call(
        margin_kernel,
        in_specs=[SMEM, SMEM] + [VMEM] * 7,
        out_specs=[VMEM, VMEM, VMEM],
        out_shape=[shape, shape, edge],
        scratch_shapes=conv_scratch(2, 6),
        compiler_params=pltpu.CompilerParams(vmem_limit_bytes=24 << 20),
        cost_estimate=pl.CostEstimate(flops=8 << 30, bytes_accessed=8 << 20, transcendentals=0),
    )(where, tissue, features, left, right, *weights)


def core_kernel(
    where_ref, tissue_ref, features_ref, mleft_ref, mright_ref, left_ref, right_ref,
    conv_ref, bias_ref, head_ref, hbias_ref,
    out_ref, prob_ref,
    logit_ref, turn_ref, factor_ref, conv_scr, head_scr, taps0, taps1, hidden0, hidden1, *buffers,
):
    tile_row, tile_col = where_ref[0], where_ref[1]
    prepare_weights(conv_ref, head_ref, conv_scr, head_scr)
    for k in range(len(buffers) // 2):
        buffers[2 * k + 1][SIDE:GAP, :] = jnp.zeros((GAP - SIDE, 128), F32)
    own_weight, side_weight = column_weights(
        tile_col, tissue_ref[0, 0], mleft_ref[0].astype(F32), mright_ref[0].astype(F32)
    )
    bias = jnp.concatenate([bias_ref[...], bias_ref[...]], axis=1)
    ray_bias = spread_bias(hbias_ref[...])
    logit_ref[...] = jnp.zeros(logit_ref.shape, F32)
    table = lax.broadcasted_iota(jnp.int32, (EXT_H, 128), 0)
    factor_ref[...] = row_weights(table, tile_row)

    def taps_stage(h, taps_ref):
        blocks = []
        for k in range(C_GROUPS + 1):
            at = C_GROUPS * h + k
            rows = [features_ref[4 * (C_FIRST + at) - 1 + r] for r in range(4)]
            blocks.append((turned(rows), left_ref[at], right_ref[at]))
        groups_taps(list(zip(blocks[:-1], blocks[1:])), buffers, taps_ref)

    def hidden_stage(taps_ref, hidden_ref):
        groups_hidden(taps_ref, hidden_ref, conv_scr, bias)

    def head_stage(h, hidden_ref):
        every = head_logits(hidden_ref, head_scr)
        for k in range(C_GROUPS):
            logits = every[k]
            for r in range(4):
                row = 4 * (C_GROUPS * h + k) + r
                rays = weighted_rays(
                    logits, r, ray_bias, own_weight, side_weight, MARGIN + row, factor_ref
                )
                start = 128 * C_GROUPS * h + 256 * (k // 2) + 4 * (k % 2) + r
                out_ref[pl.ds(start, 32, stride=8), :] = rays
                keep_probability(logit_ref, logits, r, row)

    walk(
        64 // C_GROUPS, taps_stage, hidden_stage, head_stage, (taps0, taps1), (hidden0, hidden1)
    )
    for block in range(2):
        probability_by_row(
            logit_ref, 4 * block, 4, MARGIN + 128 * block, hbias_ref[0, 0], tile_row,
            own_weight, side_weight, turn_ref,
        )
        prob_ref[block] = turn_ref[...]


def core_outputs(where, tissue, features, mleft, mright, left, right, weights):
    flag = pl.BlockSpec((1, SIDE, 128), lambda s: (M_BLOCKS, 0, 0))
    return pl.pallas_call(
        core_kernel,
        grid=(1,),
        in_specs=[SMEM, SMEM, VMEM, flag, flag] + [VMEM] * 6,
        out_specs=[VMEM, VMEM],
        out_shape=[
            jax.ShapeDtypeStruct((CORE_H * 32, 128), F32),
            jax.ShapeDtypeStruct((2, CORE_W, 128), F32),
        ],
        scratch_shapes=conv_scratch(C_GROUPS, 8),
        compiler_params=pltpu.CompilerParams(vmem_limit_bytes=32 << 20),
        cost_estimate=pl.CostEstimate(flops=16 << 30, bytes_accessed=12 << 20, transcendentals=0),
    )(where, tissue, features, mleft, mright, left, right, *weights)


def probability_kernel(
    where_ref, prob_ref, edge_ref, above_ref, below_ref,
    probability_ref, wide_ref, west_ref, east_ref,
):
    tile_row = where_ref[0]
    lane = lanes_of((CORE_W, 128))
    above = above_ref[0:128, :].astype(F32) + above_ref[128:256, :].astype(F32)
    below = below_ref[0:128, :].astype(F32) + below_ref[128:256, :].astype(F32)
    first = prob_ref[0] + jnp.where(lane < 64, pltpu.roll(above, 120, 1), 0.0)
    last = prob_ref[1] + jnp.where(lane >= 64, pltpu.roll(below, 64, 1), 0.0)
    probability_ref[0:128, :] = first.T
    probability_ref[128:256, :] = last.T
    head = pltpu.roll(above, 122, 1) + pltpu.roll(edge_ref[0], 66, 1)
    head = jnp.where(tile_row > 0, head, 0.0)
    tail = pltpu.roll(edge_ref[1], 122, 1) + pltpu.roll(below, 66, 1)
    tail = jnp.where(tile_row < N_ROWS - 1, tail, 0.0)
    first_moved, last_moved = pltpu.roll(first, 2, 1), pltpu.roll(last, 2, 1)
    parts = [
        jnp.where(lane < 2, head, first_moved),
        jnp.where(lane < 2, first_moved, last_moved),
        jnp.where(lane < 2, last_moved, jnp.where(lane < 4, tail, 0.0)),
    ]
    for k, part in enumerate(parts):
        wide_ref[:, 128 * k : 128 * (k + 1)] = part
        west_ref[:, 128 * k : 128 * (k + 1)] = part[0:8]
        east_ref[:, 128 * k : 128 * (k + 1)] = part[120:128]


def final_probability(where, prob, edge, above, below):
    last = pl.BlockSpec((256, 128), lambda s: (8, 0))
    return pl.pallas_call(
        probability_kernel,
        grid=(1,),
        in_specs=[SMEM, VMEM, VMEM, last, last],
        out_specs=[VMEM] * 4,
        out_shape=[
            jax.ShapeDtypeStruct((CORE_H, CORE_W), F32),
            jax.ShapeDtypeStruct((CORE_W, 384), F32),
            jax.ShapeDtypeStruct((8, 384), F32),
            jax.ShapeDtypeStruct((8, 384), F32),
        ],
        cost_estimate=pl.CostEstimate(flops=0, bytes_accessed=1 << 20, transcendentals=0),
    )(where, prob, edge, above, below)


def add_margins_kernel(rays_ref, above_ref, below_ref, out_ref, edge_ref, sems):
    ends = (0, 6144)
    loads = [
        pltpu.make_async_copy(rays_ref.at[pl.ds(start, 2048)], edge_ref.at[k], sems.at[k])
        for k, start in enumerate(ends)
    ]
    for load in loads:
        load.start()
    stores = []
    for k, (start, ref) in enumerate(zip(ends, (above_ref, below_ref))):
        loads[k].wait()

        def step(t, carry, k=k, ref=ref):
            for r in range(8):
                margin = ref[pl.ds(pl.multiple_of((8 * t + r) * 32, 32), 32), :].astype(F32)
                edge_ref[k, pl.ds(256 * t + r, 32, stride=8), :] += margin
            return carry

        lax.fori_loop(0, 8, step, 0, unroll=4)
        store = pltpu.make_async_copy(edge_ref.at[k], out_ref.at[pl.ds(start, 2048)], sems.at[2 + k])
        store.start()
        stores.append(store)
    for store in stores:
        store.wait()


def add_margins(rays, above, below):
    some = pl.BlockSpec(memory_space=pl.ANY)
    return pl.pallas_call(
        add_margins_kernel,
        in_specs=[some, VMEM, VMEM],
        out_specs=some,
        out_shape=jax.ShapeDtypeStruct((CORE_H * 32, 128), F32),
        scratch_shapes=[pltpu.VMEM((2, 2048, 128), F32), pltpu.SemaphoreType.DMA((4,))],
        input_output_aliases={0: 0},
        cost_estimate=pl.CostEstimate(flops=0, bytes_accessed=6 << 20, transcendentals=0),
    )(rays, above, below)


def peak_kernel(wide_ref, west_ref, east_ref, gap_ref, tall_ref):
    tall_ref[0:8, :] = west_ref[...]
    tall_ref[8:136, :] = wide_ref[...]
    tall_ref[136:144, :] = east_ref[...]
    best = tall_ref[6:134, :]
    for k in range(1, 5):
        best = jnp.maximum(best, tall_ref[6 + k : 134 + k, :])
    along = best
    for k in range(1, 5):
        along = jnp.maximum(along, pltpu.roll(best, 384 - k, 1))
    gap = along - pltpu.roll(wide_ref[...], 382, 1)
    gap_ref[0:128, :] = gap[:, 0:128].T
    gap_ref[128:256, :] = gap[:, 128:256].T


def peak(wide, west, east):
    return pl.pallas_call(
        peak_kernel,
        in_specs=[VMEM] * 3,
        out_specs=VMEM,
        out_shape=jax.ShapeDtypeStruct((CORE_H, CORE_W), F32),
        scratch_shapes=[pltpu.VMEM((144, 384), F32)],
    )(wide, west, east)


def shift(array, axis, step):
    count = lax.axis_size(axis)
    pairs = [(i, i + step) for i in range(count) if 0 <= i + step < count]
    return lax.ppermute(array, axis, pairs)


def body(features, conv_weight, conv_bias, head_weight, head_bias, tissue):
    features = jnp.transpose(features, (0, 2, 1))
    where = jnp.stack([lax.axis_index("rows"), lax.axis_index("cols")]).astype(jnp.int32)
    hbias = jnp.pad(head_bias[None, :], ((0, 7), (0, 128 - head_bias.shape[0])))
    weights = (
        conv_weight.reshape(9 * CIN, COUT), conv_bias[None, :], jnp.transpose(head_weight), hbias,
    )
    to_right, to_left = turn_margin(tissue, features)
    mleft = shift(to_right, "cols", 1)
    mright = shift(to_left, "cols", -1)
    to_right, to_left = turn_core(features)
    cleft = shift(to_right, "cols", 1)
    cright = shift(to_left, "cols", -1)
    up, down, edge = margin_outputs(where, tissue, features, mleft, mright, weights)
    above = shift(down, "rows", 1)
    below = shift(up, "rows", -1)
    rays, prob = core_outputs(where, tissue, features, mleft, mright, cleft, cright, weights)
    probability, wide, west, east = final_probability(where, prob, edge, above, below)
    from_west = shift(east, "cols", 1)
    from_east = shift(west, "cols", -1)
    out = add_margins(rays, above, below)
    gap = peak(wide, from_west, from_east)
    lengths = out.reshape(32, 32, 8, 128).transpose(0, 2, 1, 3).reshape(CORE_H, CORE_W * RAYS)
    return (probability, lengths, gap)


def solution(mesh):
    in_specs = (P("rows", "cols", None), P(), P(), P(), P(), P("rows", "cols"))
    out_specs = (P("rows", "cols"), P("rows", "cols"), P("rows", "cols"))
    return jax.shard_map(body, mesh=mesh, in_specs=in_specs, out_specs=out_specs, check_vma=False)
```

```python
import jax
import jax.numpy as jnp
from jax import lax
from jax.experimental import pallas as pl
from jax.experimental.pallas import tpu as pltpu
from jax.sharding import PartitionSpec as P

MARGIN = 64
EXT_H, EXT_W = 384, 256
CORE_H, CORE_W = 256, 128
N_ROWS, N_COLS = 8, 16
CIN, COUT, RAYS = 32, 128, 32
SIDE = 80
M_HALF = 19
M_BLOCKS = 2 * M_HALF
C_FIRST = 16
C_BLOCKS = 65
M_GROUPS = 18
M_OUT = 4 * M_GROUPS
GAP = 88
F32, BF16 = jnp.float32, jnp.bfloat16
SMEM = pl.BlockSpec(memory_space=pltpu.SMEM)
VMEM = pl.BlockSpec(memory_space=pltpu.VMEM)
HBM = pl.BlockSpec(memory_space=pltpu.HBM)


def lanes_of(shape):
    return lax.broadcasted_iota(jnp.int32, shape, len(shape) - 1)


def gauss(position, extent):
    spread = extent / 4.0
    centred = position.astype(F32) - (extent - 1) / 2.0
    return jnp.exp(-(centred * centred) / (2.0 * spread * spread))


def turn(rows, index, right_ref, left_ref):
    block = jnp.concatenate(rows, axis=0).T
    right_ref[index] = block[EXT_W - SIDE :]
    left_ref[index] = block[:SIDE]


def turn_margin_kernel(tissue_ref, top_ref, bottom_ref, right_ref, left_ref):
    zero = jnp.zeros((CIN, EXT_W), BF16)
    turn([zero] + [top_ref[k] for k in range(3)], 0, right_ref, left_ref)
    turn([bottom_ref[95], zero, zero, zero], M_BLOCKS - 1, right_ref, left_ref)

    def step(m, carry):
        rows = [top_ref[4 * m - 1 + k] for k in range(4)]
        turn(rows, m, right_ref, left_ref)
        rows = [bottom_ref[19 + 4 * m + k] for k in range(4)]
        turn(rows, M_HALF - 1 + m, right_ref, left_ref)
        return carry

    lax.fori_loop(1, M_HALF, step, 0, unroll=6)
    flag = jnp.where(tissue_ref[0, 0] > 0, 1.0, 0.0)
    flags = jnp.full((SIDE, 128), flag, F32).astype(BF16)
    right_ref[M_BLOCKS] = flags
    left_ref[M_BLOCKS] = flags


def turn_margin(tissue, features):
    side = jax.ShapeDtypeStruct((M_BLOCKS + 1, SIDE, 128), BF16)
    return pl.pallas_call(
        turn_margin_kernel,
        grid=(1,),
        in_specs=[
            SMEM,
            pl.BlockSpec((96, CIN, EXT_W), lambda s: (0, 0, 0)),
            pl.BlockSpec((96, CIN, EXT_W), lambda s: (3, 0, 0)),
        ],
        out_specs=[VMEM, VMEM],
        out_shape=[side, side],
        compiler_params=pltpu.CompilerParams(vmem_limit_bytes=60 << 20),
        cost_estimate=pl.CostEstimate(flops=0, bytes_accessed=8 << 20, transcendentals=0),
    )(tissue, features, features)


def turn_core_kernel(features_ref, right_ref, left_ref):
    def step(m, carry):
        rows = [features_ref[4 * (C_FIRST + m) - 1 + k] for k in range(4)]
        turn(rows, m, right_ref, left_ref)
        return carry

    lax.fori_loop(0, C_BLOCKS, step, 0, unroll=13)


def turn_core(features):
    side = jax.ShapeDtypeStruct((C_BLOCKS, SIDE, 128), BF16)
    return pl.pallas_call(
        turn_core_kernel,
        in_specs=[VMEM],
        out_specs=[VMEM, VMEM],
        out_shape=[side, side],
        compiler_params=pltpu.CompilerParams(vmem_limit_bytes=20 << 20),
        cost_estimate=pl.CostEstimate(flops=0, bytes_accessed=12 << 20, transcendentals=0),
    )(features)


def prepare_weights(conv_ref, head_ref, conv_scr, head_scr):
    zero = jnp.zeros((CIN, COUT), BF16)
    for o in range(2):
        for i in range(4):
            for dc in range(3):
                dr = i - o
                piece = zero
                if 0 <= dr < 3:
                    piece = conv_ref[(3 * dr + dc) * CIN : (3 * dr + dc + 1) * CIN, :]
                row = dc * 128 + i * CIN
                conv_scr[row : row + CIN, o * COUT : (o + 1) * COUT] = piece
    head = head_ref[...].astype(F32)
    head = jnp.concatenate([head, jnp.zeros((COUT - head.shape[0], COUT), F32)], axis=0).T
    part = lax.div(lanes_of((COUT, 128)), RAYS)
    first = jnp.broadcast_to(head[:, 0:1], (COUT, 128))
    for b in range(4):
        rays = jnp.where(part == b, pltpu.roll(head, (b * RAYS - 1) % 128, 1), 0.0)
        prob = jnp.where(part == b, first, 0.0)
        head_scr[b * COUT : (b + 1) * COUT, 0:128] = rays.astype(BF16)
        head_scr[b * COUT : (b + 1) * COUT, 128:256] = prob.astype(BF16)


def spread_bias(head_bias):
    part = lax.div(lanes_of((8, 128)), RAYS)
    rays = jnp.zeros((8, 128), F32)
    for b in range(4):
        rays = jnp.where(part == b, pltpu.roll(head_bias, (b * RAYS - 1) % 128, 1), rays)
    return rays[0:1]


def column_weights(tile_col, tissue, left_flags, right_flags):
    q = lax.broadcasted_iota(jnp.int32, (32, 128), 0) * 4 + lax.div(lanes_of((32, 128)), RAYS)
    own = gauss(q + MARGIN, EXT_W)
    west_side = q < MARGIN
    side = jnp.where(west_side, gauss(q + CORE_W + MARGIN, EXT_W), gauss(q - MARGIN, EXT_W))
    has_west = jnp.where(tile_col > 0, 1.0, 0.0)
    has_east = jnp.where(tile_col < N_COLS - 1, 1.0, 0.0)
    total = own + side * jnp.where(west_side, has_west, has_east)
    flags = jnp.concatenate([left_flags[:16], right_flags[:16]], axis=0)
    return own / total * jnp.where(tissue > 0, 1.0, 0.0), side / total * flags


def row_weights(row, tile_row):
    own = gauss(row, EXT_H)
    above = gauss(row + CORE_H, EXT_H) * jnp.where(tile_row > 0, 1.0, 0.0)
    below = gauss(row - CORE_H, EXT_H) * jnp.where(tile_row < N_ROWS - 1, 1.0, 0.0)
    total = own + jnp.where(row < 2 * MARGIN, above, 0.0) + jnp.where(row >= CORE_H, below, 0.0)
    return own / total


def slid(now, later):
    low_half = lanes_of(now.shape) < 64
    return pltpu.roll(jnp.where(low_half, later, now), 64, 1)


def window_taps(own, left, right, own_f, side_f, taps_ref, w):
    own_f[...] = own.astype(F32)
    side_f[0:SIDE, :] = left.astype(F32)
    side_f[GAP : GAP + SIDE, :] = right.astype(F32)
    for d in range(3):
        lanes = slice(128 * d, 128 * (d + 1))
        for b in range(4):
            row = 256 * w + 32 * b
            taps_ref[row : row + 32, lanes] = own_f[pl.ds(15 + b + d, 32, stride=4), :].astype(BF16)
            west = side_f[pl.ds(15 + b + d, 16, stride=4), :]
            east = side_f[pl.ds(GAP - 1 + b + d, 16, stride=4), :]
            taps_ref[row + 128 : row + 144, lanes] = west.astype(BF16)
            taps_ref[row + 144 : row + 160, lanes] = east.astype(BF16)


def turned(rows):
    return jnp.concatenate(rows, axis=0).T[48:208]


def groups_taps(sources, buffers, taps_ref):
    for k, (now, later) in enumerate(sources):
        windows = now, tuple(slid(x, y) for x, y in zip(now, later))
        for w, window in enumerate(windows):
            at = 2 * k + w
            window_taps(*window, buffers[2 * at], buffers[2 * at + 1], taps_ref, at)


def groups_hidden(taps_ref, hidden_ref, conv_scr, bias):
    for first in range(0, taps_ref.shape[0], CONV_CHUNK):
        summed = jnp.dot(
            taps_ref[first : first + CONV_CHUNK, :], conv_scr[...], preferred_element_type=F32
        )
        hidden = jnp.maximum(summed + bias, 0.0).astype(BF16)
        for w in range(CONV_CHUNK // 256):
            for o in range(2):
                for s in range(2):
                    row = first // 2 + 32 * (4 * w + 2 * o + s)
                    for b in range(4):
                        start = 256 * w + 128 * s + 32 * b
                        hidden_ref[row : row + 32, b * COUT : (b + 1) * COUT] = hidden[
                            start : start + 32, o * COUT : (o + 1) * COUT
                        ]


def head_logits(hidden_ref, head_scr):
    every = []
    for first in range(0, hidden_ref.shape[0], HEAD_CHUNK):
        logits = jnp.dot(
            hidden_ref[first : first + HEAD_CHUNK, :], head_scr[...], preferred_element_type=F32
        )
        every += [logits[k : k + 256] for k in range(0, HEAD_CHUNK, 256)]
    return every


def walk(count, taps_stage, hidden_stage, head_stage, taps, hidden, after=None):
    taps_stage(0, taps[0])
    taps_stage(1, taps[1])
    hidden_stage(taps[0], hidden[0])

    def two(n, carry):
        for odd in (1, 0):
            i = 2 * n + 2 - odd
            taps_stage(i + 1, taps[1 - odd])
            hidden_stage(taps[odd], hidden[odd])
            head_stage(i - 1, hidden[1 - odd])
        if after is not None:
            after(n)
        return carry

    lax.fori_loop(0, (count - 2) // 2, two, 0)
    head_stage(count - 2, hidden[0])
    hidden_stage(taps[1], hidden[1])
    head_stage(count - 1, hidden[1])


def split_logits(logits, r):
    return logits[64 * r : 64 * r + 32], logits[64 * r + 32 : 64 * r + 64]


def weighted_rays(logits, r, ray_bias, own_weight, side_weight, row, factor_ref):
    own, side = split_logits(logits, r)
    factor = factor_ref[pl.ds(row, 1), :]
    return (
        (own[:, :128] + ray_bias) * own_weight + (side[:, :128] + ray_bias) * side_weight
    ) * factor


def keep_probability(logit_ref, logits, r, position):
    spot = lax.rem(lanes_of((32, 128)), RAYS) == lax.rem(position, RAYS)
    block = lax.div(position, RAYS)
    for k, part in enumerate(split_logits(logits, r)):
        logit_ref[k, block] = jnp.where(spot, part[:, 128:], logit_ref[k, block])


def probability_by_row(logit_ref, first_block, blocks, first_row, bias, tile_row, own_weight, side_weight, out_ref):
    lane = lanes_of((32, 128))
    values = []
    for j in range(blocks):
        own = 1.0 / (1.0 + jnp.exp(-(logit_ref[0, first_block + j] + bias)))
        side = 1.0 / (1.0 + jnp.exp(-(logit_ref[1, first_block + j] + bias)))
        factor = row_weights(first_row + 32 * j + lax.rem(lane, RAYS), tile_row)
        values.append((own * own_weight + side * side_weight) * factor)
    for b in range(4):
        rows = jnp.zeros((32, 128), F32)
        for j in range(blocks):
            moved = values[j] if j == b else pltpu.roll(values[j], ((j - b) * 32) % 128, 1)
            rows = jnp.where(lax.div(lane, 32) == j, moved, rows)
        out_ref[pl.ds(b, 32, stride=4), :] = rows


def margin_kernel(
    where_ref, tissue_ref, features_hbm, left_ref, right_ref, conv_ref, bias_ref, head_ref, hbias_ref,
    up_ref, down_ref, edge_ref,
    features_ref, load_sems,
    logit_ref, turn_ref, factor_ref, conv_scr, head_scr, taps0, taps1, hidden0, hidden1, *buffers,
):
    tile_row, tile_col = where_ref[0], where_ref[1]
    loads = [
        pltpu.make_async_copy(features_hbm.at[rows], features_ref.at[rows], load_sems.at[k])
        for k, rows in enumerate((pl.ds(0, 80), pl.ds(EXT_H - 80, 80)))
    ]
    for load in loads:
        load.start()
    prepare_weights(conv_ref, head_ref, conv_scr, head_scr)
    for k in range(len(buffers) // 2):
        buffers[2 * k + 1][SIDE:GAP, :] = jnp.zeros((GAP - SIDE, 128), F32)
    own_weight, side_weight = column_weights(
        tile_col, tissue_ref[0, 0], left_ref[M_BLOCKS].astype(F32), right_ref[M_BLOCKS].astype(F32)
    )
    bias = jnp.concatenate([bias_ref[...], bias_ref[...]], axis=1)
    ray_bias = spread_bias(hbias_ref[...])
    logit_ref[...] = jnp.zeros(logit_ref.shape, F32)
    table = lax.broadcasted_iota(jnp.int32, (EXT_H, 128), 0)
    factor_ref[...] = row_weights(table, tile_row)
    for load in loads:
        load.wait()

    def taps_stage(g, taps_ref):
        def source(first_block, first_row, block):
            rows = []
            for k in range(4):
                row = first_row + 4 * block - 1 + k
                inside = (row >= 0) & (row < EXT_H)
                values = features_ref[jnp.where(inside, row, 0)]
                rows.append(jnp.where(inside, values, jnp.zeros_like(values)))
            at = first_block + block
            return turned(rows), left_ref[at], right_ref[at]

        groups_taps(
            [
                (source(*half, g), source(*half, g + 1))
                for half in ((0, 0), (M_HALF, EXT_H - M_OUT))
            ],
            buffers, taps_ref,
        )

    def hidden_stage(taps_ref, hidden_ref):
        groups_hidden(taps_ref, hidden_ref, conv_scr, bias)

    def head_stage(g, hidden_ref):
        every = head_logits(hidden_ref, head_scr)
        for half, (ref, first_row) in enumerate(((up_ref, 0), (down_ref, EXT_H - M_OUT))):
            logits = every[half]
            for r in range(4):
                position = 4 * g + r
                rays = weighted_rays(
                    logits, r, ray_bias, own_weight, side_weight, first_row + position, factor_ref
                )
                slot = position
                if half == 1:
                    slot = jnp.where(position < 8, position + 64, position - 8)
                ref[pl.ds(pl.multiple_of(slot * 32, 32), 32), :] = rays.astype(BF16)
                keep_probability(logit_ref, logits, r, position + 96 * half)

    walk(M_GROUPS, taps_stage, hidden_stage, head_stage, (taps0, taps1), (hidden0, hidden1))
    for half, (ref, first_row) in enumerate(((up_ref, 0), (down_ref, EXT_H - M_OUT))):
        probability_by_row(
            logit_ref, 3 * half, 3, first_row, hbias_ref[0, 0], tile_row,
            own_weight, side_weight, turn_ref,
        )
        prob = jnp.where(lanes_of((CORE_W, 128)) < M_OUT, turn_ref[...], 0.0)
        edge_ref[half] = prob
        high = prob.astype(BF16)
        ref[2048:2176, :] = high
        ref[2176:2304, :] = (prob - high.astype(F32)).astype(BF16)


C_GROUPS = 4
CONV_CHUNK, HEAD_CHUNK = 256, 256


def conv_scratch(groups, logit_blocks):
    return [
        pltpu.VMEM((2, logit_blocks, 32, 128), F32),
        pltpu.VMEM((CORE_W, 128), F32),
        pltpu.VMEM((EXT_H, 128), F32),
        pltpu.VMEM((384, 256), BF16),
        pltpu.VMEM((4 * COUT, 256), BF16),
        pltpu.VMEM((512 * groups, 384), BF16),
        pltpu.VMEM((512 * groups, 384), BF16),
        pltpu.VMEM((256 * groups, 512), BF16),
        pltpu.VMEM((256 * groups, 512), BF16),
    ] + [pltpu.VMEM((160, 128), F32), pltpu.VMEM((GAP + SIDE, 128), F32)] * (2 * groups)


def margin_outputs(where, tissue, features, left, right, weights):
    shape = jax.ShapeDtypeStruct((2304, 128), BF16)
    edge = jax.ShapeDtypeStruct((2, CORE_W, 128), F32)
    return pl.pallas_call(
        margin_kernel,
        in_specs=[SMEM, SMEM, HBM] + [VMEM] * 6,
        out_specs=[VMEM, VMEM, VMEM],
        out_shape=[shape, shape, edge],
        scratch_shapes=[
            pltpu.VMEM((EXT_H, CIN, EXT_W), BF16), pltpu.SemaphoreType.DMA((2,)),
        ] + conv_scratch(2, 6),
        compiler_params=pltpu.CompilerParams(vmem_limit_bytes=24 << 20),
        cost_estimate=pl.CostEstimate(flops=8 << 30, bytes_accessed=8 << 20, transcendentals=0),
    )(where, tissue, features, left, right, *weights)


def core_kernel(
    where_ref, tissue_ref, features_ref, mleft_ref, mright_ref, left_ref, right_ref,
    conv_ref, bias_ref, head_ref, hbias_ref,
    out_hbm, prob_ref,
    out_ref, store_sems,
    logit_ref, turn_ref, factor_ref, conv_scr, head_scr, taps0, taps1, hidden0, hidden1, *buffers,
):
    tile_row, tile_col = where_ref[0], where_ref[1]
    prepare_weights(conv_ref, head_ref, conv_scr, head_scr)
    for k in range(len(buffers) // 2):
        buffers[2 * k + 1][SIDE:GAP, :] = jnp.zeros((GAP - SIDE, 128), F32)
    own_weight, side_weight = column_weights(
        tile_col, tissue_ref[0, 0], mleft_ref[0].astype(F32), mright_ref[0].astype(F32)
    )
    bias = jnp.concatenate([bias_ref[...], bias_ref[...]], axis=1)
    ray_bias = spread_bias(hbias_ref[...])
    logit_ref[...] = jnp.zeros(logit_ref.shape, F32)
    table = lax.broadcasted_iota(jnp.int32, (EXT_H, 128), 0)
    factor_ref[...] = row_weights(table, tile_row)

    def taps_stage(h, taps_ref):
        blocks = []
        for k in range(C_GROUPS + 1):
            at = C_GROUPS * h + k
            rows = [features_ref[4 * (C_FIRST + at) - 1 + r] for r in range(4)]
            blocks.append((turned(rows), left_ref[at], right_ref[at]))
        groups_taps(list(zip(blocks[:-1], blocks[1:])), buffers, taps_ref)

    def hidden_stage(taps_ref, hidden_ref):
        groups_hidden(taps_ref, hidden_ref, conv_scr, bias)

    def head_stage(h, hidden_ref):
        every = head_logits(hidden_ref, head_scr)
        for k in range(C_GROUPS):
            logits = every[k]
            for r in range(4):
                row = 4 * (C_GROUPS * h + k) + r
                rays = weighted_rays(
                    logits, r, ray_bias, own_weight, side_weight, MARGIN + row, factor_ref
                )
                start = 128 * C_GROUPS * h + 256 * (k // 2) + 4 * (k % 2) + r
                out_ref[pl.ds(start, 32, stride=8), :] = rays
                keep_probability(logit_ref, logits, r, row)

    stores = [
        pltpu.make_async_copy(out_ref.at[rows], out_hbm.at[rows], store_sems.at[k])
        for k, rows in enumerate((pl.ds(0, 4096), pl.ds(4096, 4096)))
    ]

    def first_half_out(n):
        @pl.when(n == 32 // C_GROUPS // 2 - 1)
        def _():
            stores[0].start()

    walk(
        64 // C_GROUPS, taps_stage, hidden_stage, head_stage, (taps0, taps1), (hidden0, hidden1),
        first_half_out,
    )
    stores[1].start()
    for block in range(2):
        probability_by_row(
            logit_ref, 4 * block, 4, MARGIN + 128 * block, hbias_ref[0, 0], tile_row,
            own_weight, side_weight, turn_ref,
        )
        prob_ref[block] = turn_ref[...]
    for store in stores:
        store.wait()


def core_outputs(where, tissue, features, mleft, mright, left, right, weights):
    flag = pl.BlockSpec((1, SIDE, 128), lambda s: (M_BLOCKS, 0, 0))
    return pl.pallas_call(
        core_kernel,
        grid=(1,),
        in_specs=[SMEM, SMEM, VMEM, flag, flag] + [VMEM] * 6,
        out_specs=[HBM, VMEM],
        out_shape=[
            jax.ShapeDtypeStruct((CORE_H * 32, 128), F32),
            jax.ShapeDtypeStruct((2, CORE_W, 128), F32),
        ],
        scratch_shapes=[
            pltpu.VMEM((CORE_H * 32, 128), F32), pltpu.SemaphoreType.DMA((2,)),
        ] + conv_scratch(C_GROUPS, 8),
        compiler_params=pltpu.CompilerParams(vmem_limit_bytes=32 << 20),
        cost_estimate=pl.CostEstimate(flops=16 << 30, bytes_accessed=12 << 20, transcendentals=0),
    )(where, tissue, features, mleft, mright, left, right, *weights)


def probability_kernel(
    where_ref, prob_ref, edge_ref, above_ref, below_ref,
    probability_ref, wide_ref, west_ref, east_ref,
):
    tile_row = where_ref[0]
    lane = lanes_of((CORE_W, 128))
    above = above_ref[0:128, :].astype(F32) + above_ref[128:256, :].astype(F32)
    below = below_ref[0:128, :].astype(F32) + below_ref[128:256, :].astype(F32)
    first = prob_ref[0] + jnp.where(lane < 64, pltpu.roll(above, 120, 1), 0.0)
    last = prob_ref[1] + jnp.where(lane >= 64, pltpu.roll(below, 64, 1), 0.0)
    probability_ref[0:128, :] = first.T
    probability_ref[128:256, :] = last.T
    head = pltpu.roll(above, 122, 1) + pltpu.roll(edge_ref[0], 66, 1)
    head = jnp.where(tile_row > 0, head, 0.0)
    tail = pltpu.roll(edge_ref[1], 122, 1) + pltpu.roll(below, 66, 1)
    tail = jnp.where(tile_row < N_ROWS - 1, tail, 0.0)
    first_moved, last_moved = pltpu.roll(first, 2, 1), pltpu.roll(last, 2, 1)
    parts = [
        jnp.where(lane < 2, head, first_moved),
        jnp.where(lane < 2, first_moved, last_moved),
        jnp.where(lane < 2, last_moved, jnp.where(lane < 4, tail, 0.0)),
    ]
    for k, part in enumerate(parts):
        wide_ref[:, 128 * k : 128 * (k + 1)] = part
        west_ref[:, 128 * k : 128 * (k + 1)] = part[0:8]
        east_ref[:, 128 * k : 128 * (k + 1)] = part[120:128]


def final_probability(where, prob, edge, above, below):
    last = pl.BlockSpec((256, 128), lambda s: (8, 0))
    return pl.pallas_call(
        probability_kernel,
        grid=(1,),
        in_specs=[SMEM, VMEM, VMEM, last, last],
        out_specs=[VMEM] * 4,
        out_shape=[
            jax.ShapeDtypeStruct((CORE_H, CORE_W), F32),
            jax.ShapeDtypeStruct((CORE_W, 384), F32),
            jax.ShapeDtypeStruct((8, 384), F32),
            jax.ShapeDtypeStruct((8, 384), F32),
        ],
        compiler_params=pltpu.CompilerParams(vmem_limit_bytes=8 << 20),
        cost_estimate=pl.CostEstimate(flops=0, bytes_accessed=1 << 20, transcendentals=0),
    )(where, prob, edge, above, below)


def add_margins_kernel(rays_ref, above_ref, below_ref, out_ref, edge_ref, sems):
    ends = (0, 6144)
    loads = [
        pltpu.make_async_copy(rays_ref.at[pl.ds(start, 2048)], edge_ref.at[k], sems.at[k])
        for k, start in enumerate(ends)
    ]
    for load in loads:
        load.start()
    stores = []
    for k, (start, ref) in enumerate(zip(ends, (above_ref, below_ref))):
        loads[k].wait()

        def step(t, carry, k=k, ref=ref):
            for r in range(8):
                margin = ref[pl.ds(pl.multiple_of((8 * t + r) * 32, 32), 32), :].astype(F32)
                edge_ref[k, pl.ds(256 * t + r, 32, stride=8), :] += margin
            return carry

        lax.fori_loop(0, 8, step, 0, unroll=4)
        store = pltpu.make_async_copy(edge_ref.at[k], out_ref.at[pl.ds(start, 2048)], sems.at[2 + k])
        store.start()
        stores.append(store)
    for store in stores:
        store.wait()


def add_margins(rays, above, below):
    some = pl.BlockSpec(memory_space=pl.ANY)
    return pl.pallas_call(
        add_margins_kernel,
        in_specs=[some, VMEM, VMEM],
        out_specs=some,
        out_shape=jax.ShapeDtypeStruct((CORE_H * 32, 128), F32),
        scratch_shapes=[pltpu.VMEM((2, 2048, 128), F32), pltpu.SemaphoreType.DMA((4,))],
        input_output_aliases={0: 0},
        compiler_params=pltpu.CompilerParams(vmem_limit_bytes=8 << 20),
        cost_estimate=pl.CostEstimate(flops=0, bytes_accessed=6 << 20, transcendentals=0),
    )(rays, above, below)


def peak_kernel(wide_ref, west_ref, east_ref, gap_ref, tall_ref):
    tall_ref[0:8, :] = west_ref[...]
    tall_ref[8:136, :] = wide_ref[...]
    tall_ref[136:144, :] = east_ref[...]
    best = tall_ref[6:134, :]
    for k in range(1, 5):
        best = jnp.maximum(best, tall_ref[6 + k : 134 + k, :])
    along = best
    for k in range(1, 5):
        along = jnp.maximum(along, pltpu.roll(best, 384 - k, 1))
    gap = along - pltpu.roll(wide_ref[...], 382, 1)
    gap_ref[0:128, :] = gap[:, 0:128].T
    gap_ref[128:256, :] = gap[:, 128:256].T


def peak(wide, west, east):
    return pl.pallas_call(
        peak_kernel,
        in_specs=[VMEM] * 3,
        out_specs=VMEM,
        out_shape=jax.ShapeDtypeStruct((CORE_H, CORE_W), F32),
        scratch_shapes=[pltpu.VMEM((144, 384), F32)],
        compiler_params=pltpu.CompilerParams(vmem_limit_bytes=8 << 20),
    )(wide, west, east)


def shift(array, axis, step):
    count = lax.axis_size(axis)
    pairs = [(i, i + step) for i in range(count) if 0 <= i + step < count]
    return lax.ppermute(array, axis, pairs)


def body(features, conv_weight, conv_bias, head_weight, head_bias, tissue):
    features = jnp.transpose(features, (0, 2, 1))
    where = jnp.stack([lax.axis_index("rows"), lax.axis_index("cols")]).astype(jnp.int32)
    hbias = jnp.pad(head_bias[None, :], ((0, 7), (0, 128 - head_bias.shape[0])))
    weights = (
        conv_weight.reshape(9 * CIN, COUT), conv_bias[None, :], jnp.transpose(head_weight), hbias,
    )
    to_right, to_left = turn_margin(tissue, features)
    mleft = shift(to_right, "cols", 1)
    mright = shift(to_left, "cols", -1)
    to_right, to_left = turn_core(features)
    cleft = shift(to_right, "cols", 1)
    cright = shift(to_left, "cols", -1)
    up, down, edge = margin_outputs(where, tissue, features, mleft, mright, weights)
    above = shift(down, "rows", 1)
    below = shift(up, "rows", -1)
    rays, prob = core_outputs(where, tissue, features, mleft, mright, cleft, cright, weights)
    probability, wide, west, east = final_probability(where, prob, edge, above, below)
    from_west = shift(east, "cols", 1)
    from_east = shift(west, "cols", -1)
    out = add_margins(rays, above, below)
    gap = peak(wide, from_west, from_east)
    lengths = out.reshape(32, 32, 8, 128).transpose(0, 2, 1, 3).reshape(CORE_H, CORE_W * RAYS)
    return (probability, lengths, gap)


def solution(mesh):
    in_specs = (P("rows", "cols", None), P(), P(), P(), P(), P("rows", "cols"))
    out_specs = (P("rows", "cols"), P("rows", "cols"), P("rows", "cols"))
    return jax.shard_map(body, mesh=mesh, in_specs=in_specs, out_specs=out_specs, check_vma=False)
```

```python
import jax
import jax.numpy as jnp
from jax import lax
from jax.experimental import pallas as pl
from jax.experimental.pallas import tpu as pltpu
from jax.sharding import PartitionSpec as P

MARGIN = 64
EXT_H, EXT_W = 384, 256
CORE_H, CORE_W = 256, 128
N_ROWS, N_COLS = 8, 16
CIN, COUT, RAYS = 32, 128, 32
SIDE = 80
M_HALF = 19
M_BLOCKS = 2 * M_HALF
C_FIRST = 16
C_BLOCKS = 65
M_GROUPS = 18
M_OUT = 4 * M_GROUPS
GAP = 88
F32, BF16 = jnp.float32, jnp.bfloat16
SMEM = pl.BlockSpec(memory_space=pltpu.SMEM)
VMEM = pl.BlockSpec(memory_space=pltpu.VMEM)
HBM = pl.BlockSpec(memory_space=pltpu.HBM)


def lanes_of(shape):
    return lax.broadcasted_iota(jnp.int32, shape, len(shape) - 1)


def gauss(position, extent):
    spread = extent / 4.0
    centred = position.astype(F32) - (extent - 1) / 2.0
    return jnp.exp(-(centred * centred) / (2.0 * spread * spread))


def turn(rows, index, right_ref, left_ref):
    block = jnp.concatenate(rows, axis=0).T
    right_ref[index] = block[EXT_W - SIDE :]
    left_ref[index] = block[:SIDE]


def turn_margin_kernel(tissue_ref, top_ref, bottom_ref, right_ref, left_ref):
    zero = jnp.zeros((CIN, EXT_W), BF16)
    turn([zero] + [top_ref[k] for k in range(3)], 0, right_ref, left_ref)
    turn([bottom_ref[95], zero, zero, zero], M_BLOCKS - 1, right_ref, left_ref)

    def step(m, carry):
        rows = [top_ref[4 * m - 1 + k] for k in range(4)]
        turn(rows, m, right_ref, left_ref)
        rows = [bottom_ref[19 + 4 * m + k] for k in range(4)]
        turn(rows, M_HALF - 1 + m, right_ref, left_ref)
        return carry

    lax.fori_loop(1, M_HALF, step, 0, unroll=6)
    flag = jnp.where(tissue_ref[0, 0] > 0, 1.0, 0.0)
    flags = jnp.full((SIDE, 128), flag, F32).astype(BF16)
    right_ref[M_BLOCKS] = flags
    left_ref[M_BLOCKS] = flags


def turn_margin(tissue, features):
    side = jax.ShapeDtypeStruct((M_BLOCKS + 1, SIDE, 128), BF16)
    return pl.pallas_call(
        turn_margin_kernel,
        grid=(1,),
        in_specs=[
            SMEM,
            pl.BlockSpec((96, CIN, EXT_W), lambda s: (0, 0, 0)),
            pl.BlockSpec((96, CIN, EXT_W), lambda s: (3, 0, 0)),
        ],
        out_specs=[VMEM, VMEM],
        out_shape=[side, side],
        compiler_params=pltpu.CompilerParams(vmem_limit_bytes=20 << 20),
        cost_estimate=pl.CostEstimate(flops=0, bytes_accessed=8 << 20, transcendentals=0),
    )(tissue, features, features)


def turn_core_kernel(features_ref, right_ref, left_ref):
    def step(m, carry):
        rows = [features_ref[4 * (C_FIRST + m) - 1 + k] for k in range(4)]
        turn(rows, m, right_ref, left_ref)
        return carry

    lax.fori_loop(0, C_BLOCKS, step, 0, unroll=13)


def turn_core(features):
    side = jax.ShapeDtypeStruct((C_BLOCKS, SIDE, 128), BF16)
    return pl.pallas_call(
        turn_core_kernel,
        in_specs=[VMEM],
        out_specs=[VMEM, VMEM],
        out_shape=[side, side],
        compiler_params=pltpu.CompilerParams(vmem_limit_bytes=20 << 20),
        cost_estimate=pl.CostEstimate(flops=0, bytes_accessed=12 << 20, transcendentals=0),
    )(features)


def prepare_weights(conv_ref, head_ref, conv_scr, head_scr):
    zero = jnp.zeros((CIN, COUT), BF16)
    for o in range(2):
        for i in range(4):
            for dc in range(3):
                dr = i - o
                piece = zero
                if 0 <= dr < 3:
                    piece = conv_ref[(3 * dr + dc) * CIN : (3 * dr + dc + 1) * CIN, :]
                row = dc * 128 + i * CIN
                conv_scr[row : row + CIN, o * COUT : (o + 1) * COUT] = piece
    head = head_ref[...].astype(F32)
    head = jnp.concatenate([head, jnp.zeros((COUT - head.shape[0], COUT), F32)], axis=0).T
    part = lax.div(lanes_of((COUT, 128)), RAYS)
    first = jnp.broadcast_to(head[:, 0:1], (COUT, 128))
    for b in range(4):
        rays = jnp.where(part == b, pltpu.roll(head, (b * RAYS - 1) % 128, 1), 0.0)
        prob = jnp.where(part == b, first, 0.0)
        head_scr[b * COUT : (b + 1) * COUT, 0:128] = rays.astype(BF16)
        head_scr[b * COUT : (b + 1) * COUT, 128:256] = prob.astype(BF16)


def spread_bias(head_bias):
    part = lax.div(lanes_of((8, 128)), RAYS)
    rays = jnp.zeros((8, 128), F32)
    for b in range(4):
        rays = jnp.where(part == b, pltpu.roll(head_bias, (b * RAYS - 1) % 128, 1), rays)
    return rays[0:1]


def column_weights(tile_col, tissue, left_flags, right_flags):
    q = lax.broadcasted_iota(jnp.int32, (32, 128), 0) * 4 + lax.div(lanes_of((32, 128)), RAYS)
    own = gauss(q + MARGIN, EXT_W)
    west_side = q < MARGIN
    side = jnp.where(west_side, gauss(q + CORE_W + MARGIN, EXT_W), gauss(q - MARGIN, EXT_W))
    has_west = jnp.where(tile_col > 0, 1.0, 0.0)
    has_east = jnp.where(tile_col < N_COLS - 1, 1.0, 0.0)
    total = own + side * jnp.where(west_side, has_west, has_east)
    flags = jnp.concatenate([left_flags[:16], right_flags[:16]], axis=0)
    return own / total * jnp.where(tissue > 0, 1.0, 0.0), side / total * flags


def row_weights(row, tile_row):
    own = gauss(row, EXT_H)
    above = gauss(row + CORE_H, EXT_H) * jnp.where(tile_row > 0, 1.0, 0.0)
    below = gauss(row - CORE_H, EXT_H) * jnp.where(tile_row < N_ROWS - 1, 1.0, 0.0)
    total = own + jnp.where(row < 2 * MARGIN, above, 0.0) + jnp.where(row >= CORE_H, below, 0.0)
    return own / total


def slid(now, later):
    low_half = lanes_of(now.shape) < 64
    return pltpu.roll(jnp.where(low_half, later, now), 64, 1)


def window_taps(own, left, right, own_f, side_f, taps_ref, w):
    own_f[...] = own.astype(F32)
    side_f[0:SIDE, :] = left.astype(F32)
    side_f[GAP : GAP + SIDE, :] = right.astype(F32)
    for d in range(3):
        lanes = slice(128 * d, 128 * (d + 1))
        for b in range(4):
            row = 256 * w + 32 * b
            taps_ref[row : row + 32, lanes] = own_f[pl.ds(15 + b + d, 32, stride=4), :].astype(BF16)
            west = side_f[pl.ds(15 + b + d, 16, stride=4), :]
            east = side_f[pl.ds(GAP - 1 + b + d, 16, stride=4), :]
            taps_ref[row + 128 : row + 144, lanes] = west.astype(BF16)
            taps_ref[row + 144 : row + 160, lanes] = east.astype(BF16)


def turned(rows):
    return jnp.concatenate(rows, axis=0).T[48:208]


def groups_taps(sources, buffers, taps_ref):
    for k, (now, later) in enumerate(sources):
        windows = now, tuple(slid(x, y) for x, y in zip(now, later))
        for w, window in enumerate(windows):
            at = 2 * k + w
            window_taps(*window, buffers[2 * at], buffers[2 * at + 1], taps_ref, at)


def groups_hidden(taps_ref, hidden_ref, conv_scr, bias):
    for first in range(0, taps_ref.shape[0], CONV_CHUNK):
        summed = jnp.dot(
            taps_ref[first : first + CONV_CHUNK, :], conv_scr[...], preferred_element_type=F32
        )
        hidden = jnp.maximum(summed + bias, 0.0).astype(BF16)
        for w in range(CONV_CHUNK // 256):
            for o in range(2):
                for s in range(2):
                    row = first // 2 + 32 * (4 * w + 2 * o + s)
                    for b in range(4):
                        start = 256 * w + 128 * s + 32 * b
                        hidden_ref[row : row + 32, b * COUT : (b + 1) * COUT] = hidden[
                            start : start + 32, o * COUT : (o + 1) * COUT
                        ]


def head_logits(hidden_ref, head_scr):
    every = []
    for first in range(0, hidden_ref.shape[0], HEAD_CHUNK):
        logits = jnp.dot(
            hidden_ref[first : first + HEAD_CHUNK, :], head_scr[...], preferred_element_type=F32
        )
        every += [logits[k : k + 256] for k in range(0, HEAD_CHUNK, 256)]
    return every


def walk(count, taps_stage, hidden_stage, head_stage, taps, hidden, after=None):
    taps_stage(0, taps[0])
    taps_stage(1, taps[1])
    hidden_stage(taps[0], hidden[0])

    def two(n, carry):
        for odd in (1, 0):
            i = 2 * n + 2 - odd
            taps_stage(i + 1, taps[1 - odd])
            hidden_stage(taps[odd], hidden[odd])
            head_stage(i - 1, hidden[1 - odd])
        if after is not None:
            after(n)
        return carry

    lax.fori_loop(0, (count - 2) // 2, two, 0)
    head_stage(count - 2, hidden[0])
    hidden_stage(taps[1], hidden[1])
    head_stage(count - 1, hidden[1])


def split_logits(logits, r):
    return logits[64 * r : 64 * r + 32], logits[64 * r + 32 : 64 * r + 64]


def weighted_rays(logits, r, ray_bias, own_weight, side_weight, row, factor_ref):
    own, side = split_logits(logits, r)
    factor = factor_ref[pl.ds(row, 1), :]
    return (
        (own[:, :128] + ray_bias) * own_weight + (side[:, :128] + ray_bias) * side_weight
    ) * factor


def keep_probability(logit_ref, logits, r, position):
    spot = lax.rem(lanes_of((32, 128)), RAYS) == lax.rem(position, RAYS)
    block = lax.div(position, RAYS)
    for k, part in enumerate(split_logits(logits, r)):
        logit_ref[k, block] = jnp.where(spot, part[:, 128:], logit_ref[k, block])


def probability_by_row(logit_ref, first_block, blocks, first_row, bias, tile_row, own_weight, side_weight, out_ref):
    lane = lanes_of((32, 128))
    values = []
    for j in range(blocks):
        own = 1.0 / (1.0 + jnp.exp(-(logit_ref[0, first_block + j] + bias)))
        side = 1.0 / (1.0 + jnp.exp(-(logit_ref[1, first_block + j] + bias)))
        factor = row_weights(first_row + 32 * j + lax.rem(lane, RAYS), tile_row)
        values.append((own * own_weight + side * side_weight) * factor)
    for b in range(4):
        rows = jnp.zeros((32, 128), F32)
        for j in range(blocks):
            moved = values[j] if j == b else pltpu.roll(values[j], ((j - b) * 32) % 128, 1)
            rows = jnp.where(lax.div(lane, 32) == j, moved, rows)
        out_ref[pl.ds(b, 32, stride=4), :] = rows


def margin_kernel(
    where_ref, tissue_ref, features_hbm, left_ref, right_ref, conv_ref, bias_ref, head_ref, hbias_ref,
    up_ref, down_ref, edge_ref,
    features_ref, load_sems,
    logit_ref, turn_ref, factor_ref, conv_scr, head_scr, taps0, taps1, hidden0, hidden1, *buffers,
):
    tile_row, tile_col = where_ref[0], where_ref[1]
    loads = [
        pltpu.make_async_copy(features_hbm.at[rows], features_ref.at[rows], load_sems.at[k])
        for k, rows in enumerate((pl.ds(0, 80), pl.ds(EXT_H - 80, 80)))
    ]
    for load in loads:
        load.start()
    prepare_weights(conv_ref, head_ref, conv_scr, head_scr)
    for k in range(len(buffers) // 2):
        buffers[2 * k + 1][SIDE:GAP, :] = jnp.zeros((GAP - SIDE, 128), F32)
    own_weight, side_weight = column_weights(
        tile_col, tissue_ref[0, 0], left_ref[M_BLOCKS].astype(F32), right_ref[M_BLOCKS].astype(F32)
    )
    bias = jnp.concatenate([bias_ref[...], bias_ref[...]], axis=1)
    ray_bias = spread_bias(hbias_ref[...])
    logit_ref[...] = jnp.zeros(logit_ref.shape, F32)
    table = lax.broadcasted_iota(jnp.int32, (EXT_H, 128), 0)
    factor_ref[...] = row_weights(table, tile_row)
    for load in loads:
        load.wait()

    def taps_stage(g, taps_ref):
        def source(first_block, first_row, block):
            rows = []
            for k in range(4):
                row = first_row + 4 * block - 1 + k
                inside = (row >= 0) & (row < EXT_H)
                values = features_ref[jnp.where(inside, row, 0)]
                rows.append(jnp.where(inside, values, jnp.zeros_like(values)))
            at = first_block + block
            return turned(rows), left_ref[at], right_ref[at]

        groups_taps(
            [
                (source(*half, g), source(*half, g + 1))
                for half in ((0, 0), (M_HALF, EXT_H - M_OUT))
            ],
            buffers, taps_ref,
        )

    def hidden_stage(taps_ref, hidden_ref):
        groups_hidden(taps_ref, hidden_ref, conv_scr, bias)

    def head_stage(g, hidden_ref):
        every = head_logits(hidden_ref, head_scr)
        for half, (ref, first_row) in enumerate(((up_ref, 0), (down_ref, EXT_H - M_OUT))):
            logits = every[half]
            for r in range(4):
                position = 4 * g + r
                rays = weighted_rays(
                    logits, r, ray_bias, own_weight, side_weight, first_row + position, factor_ref
                )
                slot = position
                if half == 1:
                    slot = jnp.where(position < 8, position + 64, position - 8)
                ref[pl.ds(pl.multiple_of(slot * 32, 32), 32), :] = rays.astype(BF16)
                keep_probability(logit_ref, logits, r, position + 96 * half)

    walk(M_GROUPS, taps_stage, hidden_stage, head_stage, (taps0, taps1), (hidden0, hidden1))
    for half, (ref, first_row) in enumerate(((up_ref, 0), (down_ref, EXT_H - M_OUT))):
        probability_by_row(
            logit_ref, 3 * half, 3, first_row, hbias_ref[0, 0], tile_row,
            own_weight, side_weight, turn_ref,
        )
        prob = jnp.where(lanes_of((CORE_W, 128)) < M_OUT, turn_ref[...], 0.0)
        edge_ref[half] = prob
        high = prob.astype(BF16)
        ref[2048:2176, :] = high
        ref[2176:2304, :] = (prob - high.astype(F32)).astype(BF16)


C_GROUPS = 4
CONV_CHUNK, HEAD_CHUNK = 256, 256


def conv_scratch(groups, logit_blocks):
    return [
        pltpu.VMEM((2, logit_blocks, 32, 128), F32),
        pltpu.VMEM((CORE_W, 128), F32),
        pltpu.VMEM((EXT_H, 128), F32),
        pltpu.VMEM((384, 256), BF16),
        pltpu.VMEM((4 * COUT, 256), BF16),
        pltpu.VMEM((512 * groups, 384), BF16),
        pltpu.VMEM((512 * groups, 384), BF16),
        pltpu.VMEM((256 * groups, 512), BF16),
        pltpu.VMEM((256 * groups, 512), BF16),
    ] + [pltpu.VMEM((160, 128), F32), pltpu.VMEM((GAP + SIDE, 128), F32)] * (2 * groups)


def margin_outputs(where, tissue, features, left, right, weights):
    shape = jax.ShapeDtypeStruct((2304, 128), BF16)
    edge = jax.ShapeDtypeStruct((2, CORE_W, 128), F32)
    return pl.pallas_call(
        margin_kernel,
        in_specs=[SMEM, SMEM, HBM] + [VMEM] * 6,
        out_specs=[VMEM, VMEM, VMEM],
        out_shape=[shape, shape, edge],
        scratch_shapes=[
            pltpu.VMEM((EXT_H, CIN, EXT_W), BF16), pltpu.SemaphoreType.DMA((2,)),
        ] + conv_scratch(2, 6),
        compiler_params=pltpu.CompilerParams(vmem_limit_bytes=24 << 20),
        cost_estimate=pl.CostEstimate(flops=8 << 30, bytes_accessed=8 << 20, transcendentals=0),
    )(where, tissue, features, left, right, *weights)


def core_kernel(
    where_ref, tissue_ref, features_ref, mleft_ref, mright_ref, left_ref, right_ref,
    conv_ref, bias_ref, head_ref, hbias_ref,
    out_hbm, prob_ref,
    out_ref, store_sems,
    logit_ref, turn_ref, factor_ref, conv_scr, head_scr, taps0, taps1, hidden0, hidden1, *buffers,
):
    tile_row, tile_col = where_ref[0], where_ref[1]
    prepare_weights(conv_ref, head_ref, conv_scr, head_scr)
    for k in range(len(buffers) // 2):
        buffers[2 * k + 1][SIDE:GAP, :] = jnp.zeros((GAP - SIDE, 128), F32)
    own_weight, side_weight = column_weights(
        tile_col, tissue_ref[0, 0], mleft_ref[0].astype(F32), mright_ref[0].astype(F32)
    )
    bias = jnp.concatenate([bias_ref[...], bias_ref[...]], axis=1)
    ray_bias = spread_bias(hbias_ref[...])
    logit_ref[...] = jnp.zeros(logit_ref.shape, F32)
    table = lax.broadcasted_iota(jnp.int32, (EXT_H, 128), 0)
    factor_ref[...] = row_weights(table, tile_row)

    def taps_stage(h, taps_ref):
        blocks = []
        for k in range(C_GROUPS + 1):
            at = C_GROUPS * h + k
            rows = [features_ref[4 * (C_FIRST + at) - 1 + r] for r in range(4)]
            blocks.append((turned(rows), left_ref[at], right_ref[at]))
        groups_taps(list(zip(blocks[:-1], blocks[1:])), buffers, taps_ref)

    def hidden_stage(taps_ref, hidden_ref):
        groups_hidden(taps_ref, hidden_ref, conv_scr, bias)

    def head_stage(h, hidden_ref):
        every = head_logits(hidden_ref, head_scr)
        for k in range(C_GROUPS):
            logits = every[k]
            for r in range(4):
                row = 4 * (C_GROUPS * h + k) + r
                rays = weighted_rays(
                    logits, r, ray_bias, own_weight, side_weight, MARGIN + row, factor_ref
                )
                start = 128 * C_GROUPS * h + 256 * (k // 2) + 4 * (k % 2) + r
                out_ref[pl.ds(start, 32, stride=8), :] = rays
                keep_probability(logit_ref, logits, r, row)

    stores = [
        pltpu.make_async_copy(out_ref.at[rows], out_hbm.at[rows], store_sems.at[k])
        for k, rows in enumerate((pl.ds(0, 4096), pl.ds(4096, 4096)))
    ]

    def first_half_out(n):
        @pl.when(n == 32 // C_GROUPS // 2 - 1)
        def _():
            stores[0].start()

    walk(
        64 // C_GROUPS, taps_stage, hidden_stage, head_stage, (taps0, taps1), (hidden0, hidden1),
        first_half_out,
    )
    stores[1].start()
    for block in range(2):
        probability_by_row(
            logit_ref, 4 * block, 4, MARGIN + 128 * block, hbias_ref[0, 0], tile_row,
            own_weight, side_weight, turn_ref,
        )
        prob_ref[block] = turn_ref[...]
    for store in stores:
        store.wait()


def core_outputs(where, tissue, features, mleft, mright, left, right, weights):
    flag = pl.BlockSpec((1, SIDE, 128), lambda s: (M_BLOCKS, 0, 0))
    return pl.pallas_call(
        core_kernel,
        grid=(1,),
        in_specs=[SMEM, SMEM, VMEM, flag, flag] + [VMEM] * 6,
        out_specs=[HBM, VMEM],
        out_shape=[
            jax.ShapeDtypeStruct((CORE_H * 32, 128), F32),
            jax.ShapeDtypeStruct((2, CORE_W, 128), F32),
        ],
        scratch_shapes=[
            pltpu.VMEM((CORE_H * 32, 128), F32), pltpu.SemaphoreType.DMA((2,)),
        ] + conv_scratch(C_GROUPS, 8),
        compiler_params=pltpu.CompilerParams(vmem_limit_bytes=32 << 20),
        cost_estimate=pl.CostEstimate(flops=16 << 30, bytes_accessed=12 << 20, transcendentals=0),
    )(where, tissue, features, mleft, mright, left, right, *weights)


def probability_kernel(
    where_ref, prob_ref, edge_ref, above_ref, below_ref,
    probability_ref, wide_ref, west_ref, east_ref,
):
    tile_row = where_ref[0]
    lane = lanes_of((CORE_W, 128))
    above = above_ref[0:128, :].astype(F32) + above_ref[128:256, :].astype(F32)
    below = below_ref[0:128, :].astype(F32) + below_ref[128:256, :].astype(F32)
    first = prob_ref[0] + jnp.where(lane < 64, pltpu.roll(above, 120, 1), 0.0)
    last = prob_ref[1] + jnp.where(lane >= 64, pltpu.roll(below, 64, 1), 0.0)
    probability_ref[0:128, :] = first.T
    probability_ref[128:256, :] = last.T
    head = pltpu.roll(above, 122, 1) + pltpu.roll(edge_ref[0], 66, 1)
    head = jnp.where(tile_row > 0, head, 0.0)
    tail = pltpu.roll(edge_ref[1], 122, 1) + pltpu.roll(below, 66, 1)
    tail = jnp.where(tile_row < N_ROWS - 1, tail, 0.0)
    first_moved, last_moved = pltpu.roll(first, 2, 1), pltpu.roll(last, 2, 1)
    parts = [
        jnp.where(lane < 2, head, first_moved),
        jnp.where(lane < 2, first_moved, last_moved),
        jnp.where(lane < 2, last_moved, jnp.where(lane < 4, tail, 0.0)),
    ]
    for k, part in enumerate(parts):
        wide_ref[:, 128 * k : 128 * (k + 1)] = part
        west_ref[:, 128 * k : 128 * (k + 1)] = part[0:8]
        east_ref[:, 128 * k : 128 * (k + 1)] = part[120:128]


def final_probability(where, prob, edge, above, below):
    last = pl.BlockSpec((256, 128), lambda s: (8, 0))
    return pl.pallas_call(
        probability_kernel,
        grid=(1,),
        in_specs=[SMEM, VMEM, VMEM, last, last],
        out_specs=[VMEM] * 4,
        out_shape=[
            jax.ShapeDtypeStruct((CORE_H, CORE_W), F32),
            jax.ShapeDtypeStruct((CORE_W, 384), F32),
            jax.ShapeDtypeStruct((8, 384), F32),
            jax.ShapeDtypeStruct((8, 384), F32),
        ],
        compiler_params=pltpu.CompilerParams(vmem_limit_bytes=8 << 20),
        cost_estimate=pl.CostEstimate(flops=0, bytes_accessed=1 << 20, transcendentals=0),
    )(where, prob, edge, above, below)


def add_margins_kernel(rays_ref, above_ref, below_ref, out_ref, edge_ref, sems):
    ends = (0, 6144)
    loads = [
        pltpu.make_async_copy(rays_ref.at[pl.ds(start, 2048)], edge_ref.at[k], sems.at[k])
        for k, start in enumerate(ends)
    ]
    for load in loads:
        load.start()
    stores = []
    for k, (start, ref) in enumerate(zip(ends, (above_ref, below_ref))):
        loads[k].wait()

        def step(t, carry, k=k, ref=ref):
            for r in range(8):
                margin = ref[pl.ds(pl.multiple_of((8 * t + r) * 32, 32), 32), :].astype(F32)
                edge_ref[k, pl.ds(256 * t + r, 32, stride=8), :] += margin
            return carry

        lax.fori_loop(0, 8, step, 0, unroll=4)
        store = pltpu.make_async_copy(edge_ref.at[k], out_ref.at[pl.ds(start, 2048)], sems.at[2 + k])
        store.start()
        stores.append(store)
    for store in stores:
        store.wait()


def add_margins(rays, above, below):
    some = pl.BlockSpec(memory_space=pl.ANY)
    return pl.pallas_call(
        add_margins_kernel,
        in_specs=[some, VMEM, VMEM],
        out_specs=some,
        out_shape=jax.ShapeDtypeStruct((CORE_H * 32, 128), F32),
        scratch_shapes=[pltpu.VMEM((2, 2048, 128), F32), pltpu.SemaphoreType.DMA((4,))],
        input_output_aliases={0: 0},
        compiler_params=pltpu.CompilerParams(vmem_limit_bytes=8 << 20),
        cost_estimate=pl.CostEstimate(flops=0, bytes_accessed=6 << 20, transcendentals=0),
    )(rays, above, below)


def peak_kernel(wide_ref, west_ref, east_ref, gap_ref, tall_ref):
    tall_ref[0:8, :] = west_ref[...]
    tall_ref[8:136, :] = wide_ref[...]
    tall_ref[136:144, :] = east_ref[...]
    best = tall_ref[6:134, :]
    for k in range(1, 5):
        best = jnp.maximum(best, tall_ref[6 + k : 134 + k, :])
    along = best
    for k in range(1, 5):
        along = jnp.maximum(along, pltpu.roll(best, 384 - k, 1))
    gap = along - pltpu.roll(wide_ref[...], 382, 1)
    gap_ref[0:128, :] = gap[:, 0:128].T
    gap_ref[128:256, :] = gap[:, 128:256].T


def peak(wide, west, east):
    return pl.pallas_call(
        peak_kernel,
        in_specs=[VMEM] * 3,
        out_specs=VMEM,
        out_shape=jax.ShapeDtypeStruct((CORE_H, CORE_W), F32),
        scratch_shapes=[pltpu.VMEM((144, 384), F32)],
        compiler_params=pltpu.CompilerParams(vmem_limit_bytes=8 << 20),
    )(wide, west, east)


def shift(array, axis, step):
    count = lax.axis_size(axis)
    pairs = [(i, i + step) for i in range(count) if 0 <= i + step < count]
    return lax.ppermute(array, axis, pairs)


def body(features, conv_weight, conv_bias, head_weight, head_bias, tissue):
    features = jnp.transpose(features, (0, 2, 1))
    where = jnp.stack([lax.axis_index("rows"), lax.axis_index("cols")]).astype(jnp.int32)
    hbias = jnp.pad(head_bias[None, :], ((0, 7), (0, 128 - head_bias.shape[0])))
    weights = (
        conv_weight.reshape(9 * CIN, COUT), conv_bias[None, :], jnp.transpose(head_weight), hbias,
    )
    to_right, to_left = turn_margin(tissue, features)
    mleft = shift(to_right, "cols", 1)
    mright = shift(to_left, "cols", -1)
    to_right, to_left = turn_core(features)
    cleft = shift(to_right, "cols", 1)
    cright = shift(to_left, "cols", -1)
    up, down, edge = margin_outputs(where, tissue, features, mleft, mright, weights)
    above = shift(down, "rows", 1)
    below = shift(up, "rows", -1)
    rays, prob = core_outputs(where, tissue, features, mleft, mright, cleft, cright, weights)
    probability, wide, west, east = final_probability(where, prob, edge, above, below)
    from_west = shift(east, "cols", 1)
    from_east = shift(west, "cols", -1)
    out = add_margins(rays, above, below)
    gap = peak(wide, from_west, from_east)
    lengths = out.reshape(32, 32, 8, 128).transpose(0, 2, 1, 3).reshape(CORE_H, CORE_W * RAYS)
    return (probability, lengths, gap)


def solution(mesh):
    in_specs = (P("rows", "cols", None), P(), P(), P(), P(), P("rows", "cols"))
    out_specs = (P("rows", "cols"), P("rows", "cols"), P("rows", "cols"))
    return jax.shard_map(body, mesh=mesh, in_specs=in_specs, out_specs=out_specs, check_vma=False)
```
